512 devices in a mesh: pair: 64 (over y, x, core), panel: 8 (over z).
Axes of the slice: x: 4, y: 8, z: 8, core: 2. Of those that a mesh axis runs over, the one named last changes fastest.
Arguments:
- amplitudes: bfloat16 [1536, 8, 4096], P(('pair', 'panel')), may hold values from -6 to 6
- integrals: bfloat16 [3, 16384, 4096], P(None, 'pair', 'panel'), may hold values from -0.0546875 to 0.0546875
- residual_in: bfloat16 [1536, 16384], P(('pair', 'panel')), may hold values from -6 to 6
- kept_tiles: int32 [4, 3], replicated, may hold values from 0 to 7, as said below
Outputs:
- residual_out: bfloat16 [1536, 16384], P(('pair', 'panel'))
The draws below stay inside these ranges and needn't reach their ends.
Inputs may be any that keep to these rules, and one draw needn't show every extreme that they name: `kept_tiles`: each row names 3 different cd tile pairs; the first row names cd tile pairs 0 and 7.
All inputs are finite; a program needn't handle non-finite values.
Results may differ from the reference program's by a relative error of at most 0.0042.
Values may be sent and summed in bfloat16 or wider, within the bound.
No kernel may reach another device: no remote copies, remote signals or barrier semaphores. Data moves between devices by JAX's collectives and lax.ppermute only.
A program may use at most 128 MiB of HBM per device.

```python
import jax
import jax.numpy as jnp
from jax import lax

TW = 4096
NCD = 8
KEEP = 3
NAB = 4
AB_ALL = 16384
IJ = 1536


def draw_kept_tiles(key, part):
    key = jax.random.fold_in(key, 7)
    row_keys = jax.random.split(key, NAB)
    chosen = jax.vmap(lambda row_key: jax.random.permutation(row_key, NCD)[:KEEP])(row_keys)
    first_key = jax.random.fold_in(key, 11)
    order_key = jax.random.fold_in(key, 13)
    others = 1 + jax.random.permutation(first_key, NCD - 2)[:KEEP - 2]
    first_row = jnp.concatenate([jnp.array([0, NCD - 1], jnp.int32), others.astype(jnp.int32)])
    first_row = first_row[jax.random.permutation(order_key, KEEP)]
    chosen = chosen.astype(jnp.int32).at[0].set(first_row)
    return chosen.astype(jnp.int32)


def shard_levels(key, extent, cuts, least, high):
    loudness = 1.0
    for dim, parts in cuts:
        draws = jax.random.uniform(jax.random.fold_in(jax.random.fold_in(key, 6), dim), (parts,), jnp.float32, least / len(cuts), high / len(cuts))
        loudness = loudness * jnp.repeat(jnp.exp(draws), extent[dim] // parts).reshape((-1,) + (1,) * (len(extent) - 1 - dim))
    return loudness


def bell_draw(own_key, extent, scale, reach, shards=(), held_as=jnp.bfloat16):
    result = jax.random.normal(own_key, extent, jnp.float32) * scale
    if len(shards) > 0:
        result = shard_levels(own_key, extent, shards, -0.22, 0.18) * result
    return jnp.clip(result, min=-reach, max=reach).astype(held_as)


def setup_inputs(seed: int = 0) -> dict:
    key_of = jax.random.split(jax.random.key(seed), 5)
    return {
        "amplitudes": bell_draw(key_of[0], (IJ, NCD, TW), 1.0, 6.0, ((0, 512),)),
        "integrals": bell_draw(key_of[1], (KEEP, AB_ALL, TW), (KEEP * TW) ** -0.5, 0.0546875, ((1, 64), (2, 8))),
        "residual_in": bell_draw(key_of[2], (IJ, AB_ALL), 1.0, 6.0, ((0, 512),)),
        "kept_tiles": draw_kept_tiles(jax.random.fold_in(key_of[4], 71), 0),
    }


def reference(amplitudes, integrals, residual_in, kept_tiles):
    pieces = []
    for ab_tile in range(NAB):
        chosen = jnp.take(amplitudes, kept_tiles[ab_tile], axis=1).astype(jnp.float32)
        chosen = chosen.reshape(IJ, KEEP * TW)
        panel_block = integrals[:, ab_tile * TW:(ab_tile + 1) * TW, :].astype(jnp.float32)
        panel_block = jnp.transpose(panel_block, (0, 2, 1)).reshape(KEEP * TW, TW)
        pieces.append(jnp.dot(chosen, panel_block, precision=lax.Precision.HIGHEST, preferred_element_type=jnp.float32))
    ladder = jnp.concatenate(pieces, axis=1).astype(jnp.bfloat16)
    return (residual_in.astype(jnp.float32) + ladder.astype(jnp.float32)).astype(jnp.bfloat16)
```

```python
import jax
import jax.numpy as jnp
from jax import lax
from jax.sharding import Mesh, PartitionSpec as P

Y, X, CORE, Z = 8, 4, 2, 8


def shards(amplitudes, integrals, residual_in, kept_tiles):
    rows, tiles, width = amplitudes.shape
    keep = kept_tiles.shape[1]
    share = width // Z
    panel = lax.all_gather(integrals, ("x", "c"), axis=1, tiled=True)
    pick = jax.nn.one_hot(kept_tiles, tiles, dtype=jnp.bfloat16)
    pick = jnp.repeat(pick, Y // kept_tiles.shape[0], axis=0)
    outgoing = jnp.einsum(
        "ykt,rtzc->yzrkc",
        pick,
        amplitudes.reshape(rows, tiles, Z, share),
        preferred_element_type=jnp.float32,
    ).astype(jnp.bfloat16)
    outgoing = outgoing.reshape(Y * Z, rows, keep * share)
    incoming = lax.all_to_all(outgoing, ("y", "z"), split_axis=0, concat_axis=0, tiled=True)
    incoming = incoming.reshape(Y * Z * rows, keep, share)
    partial = jnp.einsum("mkc,kac->ma", incoming, panel, preferred_element_type=jnp.float32)
    partial = partial.astype(jnp.bfloat16).reshape(Y * Z, rows, -1)
    returned = lax.all_to_all(partial, ("y", "z"), split_axis=0, concat_axis=0, tiled=True)
    returned = returned.reshape(Y, Z, rows, -1).astype(jnp.float32)
    ladder = jnp.sum(returned, axis=1).astype(jnp.bfloat16)
    ladder = jnp.transpose(ladder, (1, 0, 2)).reshape(residual_in.shape)
    return (residual_in.astype(jnp.float32) + ladder.astype(jnp.float32)).astype(jnp.bfloat16)


def solution(mesh):
    fine = Mesh(mesh.devices.reshape(Y, X, CORE, Z), ("y", "x", "c", "z"))
    owner = ("y", "x", "c", "z")
    in_specs = (
        P(owner, None, None),
        P(None, ("y", "x", "c"), "z"),
        P(owner, None),
        P(),
    )
    return jax.shard_map(
        shards, mesh=fine, in_specs=in_specs, out_specs=P(owner, None), check_vma=False
    )
```

```python
import jax
import jax.numpy as jnp
from jax import lax
from jax.sharding import Mesh, PartitionSpec as P

Y, X, CORE, Z = 8, 4, 2, 8
LANES = 128
SWAP = ((0, 1), (1, 0))
UP = tuple((i, (i + 1) % X) for i in range(X))
DOWN = tuple((i, (i - 1) % X) for i in range(X))
ACROSS = tuple((i, (i + 2) % X) for i in range(X))


def shards(amplitudes, integrals, residual_in, kept_tiles):
    rows, tiles, width = amplitudes.shape
    keep = kept_tiles.shape[1]
    share = width // Z
    block = integrals.shape[1]
    x = lax.axis_index("x")
    core = lax.axis_index("c")

    below = lax.ppermute(integrals, "x", UP)
    above = lax.ppermute(integrals, "x", DOWN)
    far = lax.ppermute(integrals, "x", ACROSS)

    pick = jax.nn.one_hot(kept_tiles, tiles, dtype=jnp.bfloat16)
    pick = jnp.repeat(pick, Y // kept_tiles.shape[0], axis=0)
    outgoing = jnp.einsum(
        "ykt,rtzc->yzrkc",
        pick,
        amplitudes.reshape(rows, tiles, Z, share),
        preferred_element_type=jnp.float32,
    ).astype(jnp.bfloat16)
    outgoing = outgoing.reshape(Y * Z, rows * keep, share // LANES, LANES)
    mine = lax.all_to_all(outgoing, ("y", "z"), split_axis=0, concat_axis=0, tiled=True)
    mine = mine.reshape(Y * Z, rows, keep, share)
    theirs = lax.ppermute(mine, "c", SWAP)

    left = jnp.stack([mine, theirs], axis=2)

    def product(right):
        out = jnp.einsum(
            "drosc,sac->droa", left, right, preferred_element_type=jnp.float32
        )
        return out.astype(jnp.bfloat16)

    pieces = [product(p) for p in (integrals, above, far, below)]
    partial = jnp.concatenate(pieces, axis=-1)
    returned = lax.all_to_all(partial, ("y", "z"), split_axis=0, concat_axis=0, tiled=True)
    returned = returned.reshape(Y, Z, rows, CORE, X * block).astype(jnp.float32)
    ladder = jnp.sum(returned, axis=1).astype(jnp.bfloat16)
    ladder = ladder.reshape(Y, rows, CORE, X, block)
    own = ladder[:, :, 0]
    other = lax.ppermute(ladder[:, :, 1], "c", SWAP)
    low = jnp.where(core == 0, own, other)
    high = jnp.where(core == 0, other, own)
    both = jnp.stack([low, high], axis=3)
    both = jnp.roll(both, x, axis=2)
    both = jnp.transpose(both, (1, 0, 2, 3, 4)).reshape(residual_in.shape)
    return (residual_in.astype(jnp.float32) + both.astype(jnp.float32)).astype(jnp.bfloat16)


def solution(mesh):
    fine = Mesh(mesh.devices.reshape(Y, X, CORE, Z), ("y", "x", "c", "z"))
    owner = ("y", "x", "c", "z")
    in_specs = (
        P(owner, None, None),
        P(None, ("y", "x", "c"), "z"),
        P(owner, None),
        P(),
    )
    return jax.shard_map(
        shards, mesh=fine, in_specs=in_specs, out_specs=P(owner, None), check_vma=False
    )
```

```python
import jax
import jax.numpy as jnp
from jax import lax
from jax.experimental import pallas as pl
from jax.experimental.pallas import tpu as pltpu
from jax.sharding import Mesh, PartitionSpec as P

Y, X, CORE, Z = 8, 4, 2, 8
LANES = 128
SWAP = ((0, 1), (1, 0))
UP = tuple((i, (i + 1) % X) for i in range(X))
DOWN = tuple((i, (i - 1) % X) for i in range(X))
ACROSS = tuple((i, (i + 2) % X) for i in range(X))
VMEM = pl.BlockSpec(memory_space=pltpu.VMEM)
SMEM = pl.BlockSpec(memory_space=pltpu.SMEM)
GRANT = 32 * 1024 * 1024


def pick_kernel(kept_ref, amplitudes_ref, out_ref):
    tiles, keep = kept_ref.shape
    rows = amplitudes_ref.shape[0]
    repeat = Y // tiles
    for a in range(tiles):
        for k in range(keep):
            tile = kept_ref[a, k]
            for r in range(rows):
                piece = amplitudes_ref[r, tile]
                for i in range(repeat):
                    out_ref[a * repeat + i, :, r * keep + k] = piece


def pick(kept_tiles, amplitudes):
    rows, tiles, width = amplitudes.shape
    keep = kept_tiles.shape[1]
    split = amplitudes.reshape(rows, tiles, Z, width // Z // LANES, LANES)
    shape = (Y, Z, rows * keep, width // Z // LANES, LANES)
    return pl.pallas_call(
        pick_kernel,
        out_shape=jax.ShapeDtypeStruct(shape, amplitudes.dtype),
        in_specs=[SMEM, VMEM],
        out_specs=VMEM,
        cost_estimate=pl.CostEstimate(flops=10**11, bytes_accessed=10**6, transcendentals=0),
        compiler_params=pltpu.CompilerParams(vmem_limit_bytes=GRANT),
    )(kept_tiles, split)


def product_kernel(where_ref, left_ref, *refs):
    rights, out_ref = refs[:-1], refs[-1]
    peers, both, chunks, lanes = left_ref.shape
    halves, rows, _, columns = out_ref.shape
    keep, block, share = rights[0].shape
    left = [
        jnp.concatenate(
            [
                jnp.concatenate([left_ref[:, r * keep + k, c] for c in range(chunks)], axis=1)
                for r in range(rows)
            ],
            axis=0,
        )
        for k in range(keep)
    ]
    for j, right_ref in enumerate(rights):
        total = jnp.zeros((rows * peers, block), jnp.float32)
        for k in range(keep):
            total += lax.dot_general(
                left[k],
                right_ref[k],
                (((1,), (1,)), ((), ())),
                preferred_element_type=jnp.float32,
            )
        place = where_ref[j]
        per_half = columns // block
        start = pl.multiple_of(lax.rem(place, per_half) * block, block)
        out_ref[lax.div(place, per_half), :, :, pl.ds(start, block)] = total.astype(jnp.bfloat16).reshape(rows, peers, block)


def product(where, left, rights):
    peers = left.shape[0]
    rows = left.shape[1] // rights[0].shape[0]
    columns = sum(r.shape[1] for r in rights) // 2
    return pl.pallas_call(
        product_kernel,
        out_shape=jax.ShapeDtypeStruct((2, rows, peers, columns), jnp.bfloat16),
        in_specs=[SMEM] + [VMEM] * (1 + len(rights)),
        out_specs=VMEM,
        cost_estimate=pl.CostEstimate(flops=1000, bytes_accessed=1000, transcendentals=0),
        compiler_params=pltpu.CompilerParams(vmem_limit_bytes=GRANT),
    )(where, left, *rights)


def shards(amplitudes, integrals, residual_in, kept_tiles):
    rows, tiles, width = amplitudes.shape
    keep = kept_tiles.shape[1]
    share = width // Z
    x = lax.axis_index("x")
    core = lax.axis_index("c")

    below = lax.ppermute(integrals, "x", UP)
    above = lax.ppermute(integrals, "x", DOWN)
    far = lax.ppermute(integrals, "x", ACROSS)

    outgoing = pick(kept_tiles, amplitudes)
    outgoing = outgoing.reshape(Y * Z, rows * keep, share // LANES, LANES)
    mine = lax.all_to_all(outgoing, ("y", "z"), split_axis=0, concat_axis=0, tiled=True)

    ring = [integrals, above, far, below]
    rights = ring + [lax.ppermute(r, "c", SWAP) for r in ring]
    steps = jnp.arange(X)
    blocks = lax.rem(x + steps, X) * CORE
    where = jnp.concatenate([blocks + core, blocks + 1 - core])
    partial = product(where.astype(jnp.int32), mine, rights)
    partial = partial.transpose(2, 1, 0, 3)
    returned = lax.all_to_all(partial, ("y", "z"), split_axis=0, concat_axis=0, tiled=True)
    returned = returned.reshape(Y, Z, rows, -1).astype(jnp.float32)
    ladder = jnp.sum(returned, axis=1).astype(jnp.bfloat16)
    ladder = jnp.transpose(ladder, (1, 0, 2)).reshape(residual_in.shape)
    return (residual_in.astype(jnp.float32) + ladder.astype(jnp.float32)).astype(jnp.bfloat16)


def solution(mesh):
    fine = Mesh(mesh.devices.reshape(Y, X, CORE, Z), ("y", "x", "c", "z"))
    owner = ("y", "x", "c", "z")
    in_specs = (
        P(owner, None, None),
        P(None, ("y", "x", "c"), "z"),
        P(owner, None),
        P(),
    )
    return jax.shard_map(
        shards, mesh=fine, in_specs=in_specs, out_specs=P(owner, None), check_vma=False
    )
```

```python
import jax
import jax.numpy as jnp
from jax import lax
from jax.experimental import pallas as pl
from jax.experimental.pallas import tpu as pltpu
from jax.sharding import Mesh, PartitionSpec as P

Y, X, CORE, Z = 8, 4, 2, 8
LANES = 128
SWAP = ((0, 1), (1, 0))
UP = tuple((i, (i + 1) % X) for i in range(X))
DOWN = tuple((i, (i - 1) % X) for i in range(X))
VMEM = pl.BlockSpec(memory_space=pltpu.VMEM)
SMEM = pl.BlockSpec(memory_space=pltpu.SMEM)
GRANT = 32 * 1024 * 1024


def pick_kernel(kept_ref, amplitudes_ref, out_ref):
    tiles, keep = kept_ref.shape
    rows = amplitudes_ref.shape[0]
    repeat = Y // tiles
    for a in range(tiles):
        for k in range(keep):
            tile = kept_ref[a, k]
            for r in range(rows):
                piece = amplitudes_ref[r, tile]
                for i in range(repeat):
                    out_ref[a * repeat + i, :, r * keep + k] = piece


def pick(kept_tiles, amplitudes):
    rows, tiles, width = amplitudes.shape
    keep = kept_tiles.shape[1]
    split = amplitudes.reshape(rows, tiles, Z, width // Z // LANES, LANES)
    shape = (Y, Z, rows * keep, width // Z // LANES, LANES)
    return pl.pallas_call(
        pick_kernel,
        out_shape=jax.ShapeDtypeStruct(shape, amplitudes.dtype),
        in_specs=[SMEM, VMEM],
        out_specs=VMEM,
        cost_estimate=pl.CostEstimate(flops=10**11, bytes_accessed=10**6, transcendentals=0),
        compiler_params=pltpu.CompilerParams(vmem_limit_bytes=GRANT),
    )(kept_tiles, split)


def halves_kernel(below_ref, above_ref, low_ref, high_ref):
    half = low_ref.shape[1]
    low_ref[...] = below_ref[:, :half]
    high_ref[...] = above_ref[:, half:]


def halves(below, above):
    keep, block, share = below.shape
    shape = jax.ShapeDtypeStruct((keep, block // 2, share), below.dtype)
    return pl.pallas_call(
        halves_kernel,
        out_shape=(shape, shape),
        in_specs=[VMEM, VMEM],
        out_specs=(VMEM, VMEM),
        cost_estimate=pl.CostEstimate(flops=10**11, bytes_accessed=10**6, transcendentals=0),
        compiler_params=pltpu.CompilerParams(vmem_limit_bytes=GRANT),
    )(below, above)


def product_kernel(where_ref, left_ref, *refs):
    rights, out_ref = refs[:-1], refs[-1]
    peers, both, chunks, lanes = left_ref.shape
    keep, _, share = rights[0].shape
    rows = both // keep
    left = [
        jnp.concatenate(
            [
                jnp.concatenate([left_ref[:, r * keep + k, c] for c in range(chunks)], axis=1)
                for r in range(rows)
            ],
            axis=0,
        )
        for k in range(keep)
    ]
    for j, right_ref in enumerate(rights):
        block = right_ref.shape[1]
        total = jnp.zeros((rows * peers, block), jnp.float32)
        for k in range(keep):
            total += lax.dot_general(
                left[k],
                right_ref[k],
                (((1,), (1,)), ((), ())),
                preferred_element_type=jnp.float32,
            )
        start = pl.multiple_of(where_ref[j] * LANES, LANES)
        out_ref[:, :, pl.ds(start, block)] = total.astype(jnp.bfloat16).reshape(rows, peers, block)


def product(where, left, rights, work):
    peers = left.shape[0]
    rows = left.shape[1] // rights[0].shape[0]
    columns = sum(r.shape[1] for r in rights)
    return pl.pallas_call(
        product_kernel,
        out_shape=jax.ShapeDtypeStruct((rows, peers, columns), jnp.bfloat16),
        in_specs=[SMEM] + [VMEM] * (1 + len(rights)),
        out_specs=VMEM,
        cost_estimate=pl.CostEstimate(flops=work, bytes_accessed=1000, transcendentals=0),
        compiler_params=pltpu.CompilerParams(vmem_limit_bytes=GRANT),
    )(where, left, *rights)


def shards(amplitudes, integrals, residual_in, kept_tiles):
    rows, tiles, width = amplitudes.shape
    keep = kept_tiles.shape[1]
    share = width // Z
    block = integrals.shape[1]
    x = lax.axis_index("x")
    core = lax.axis_index("c")

    below = lax.ppermute(integrals, "x", UP)
    above = lax.ppermute(integrals, "x", DOWN)
    low, high = halves(below, above)
    far_low = lax.ppermute(low, "x", UP)
    far_high = lax.ppermute(high, "x", DOWN)

    outgoing = pick(kept_tiles, amplitudes)
    outgoing = outgoing.reshape(Y * Z, rows * keep, share // LANES, LANES)
    mine = lax.all_to_all(outgoing, ("y", "z"), split_axis=0, concat_axis=0, tiled=True)
    theirs = lax.ppermute(mine, "c", SWAP)

    rights = (integrals, above, below, far_low, far_high)
    steps = jnp.array([0, 1, X - 1, 2, 2], jnp.int32)
    offsets = jnp.array([0, 0, 0, 0, 1], jnp.int32)
    where = lax.rem(x.astype(jnp.int32) + steps, X) * (block // LANES) + offsets
    first = product(where, mine, rights, 10**10)
    second = product(where, theirs, rights, 1000)
    partial = jnp.stack([first, second], axis=1)
    partial = partial.transpose(2, 0, 1, 3)
    returned = lax.all_to_all(partial, ("y", "z"), split_axis=0, concat_axis=0, tiled=True)
    returned = returned.reshape(Y, Z, rows, CORE, X * block).astype(jnp.float32)
    ladder = jnp.sum(returned, axis=1).astype(jnp.bfloat16)
    ladder = ladder.reshape(Y, rows, CORE, X, block)
    own = ladder[:, :, 0]
    other = lax.ppermute(ladder[:, :, 1], "c", SWAP)
    low = jnp.where(core == 0, own, other)
    high = jnp.where(core == 0, other, own)
    both = jnp.stack([low, high], axis=3)
    both = jnp.transpose(both, (1, 0, 2, 3, 4)).reshape(residual_in.shape)
    return (residual_in.astype(jnp.float32) + both.astype(jnp.float32)).astype(jnp.bfloat16)


def solution(mesh):
    fine = Mesh(mesh.devices.reshape(Y, X, CORE, Z), ("y", "x", "c", "z"))
    owner = ("y", "x", "c", "z")
    in_specs = (
        P(owner, None, None),
        P(None, ("y", "x", "c"), "z"),
        P(owner, None),
        P(),
    )
    return jax.shard_map(
        shards, mesh=fine, in_specs=in_specs, out_specs=P(owner, None), check_vma=False
    )
```

```python
import jax
import jax.numpy as jnp
from jax import lax
from jax.experimental import pallas as pl
from jax.experimental.pallas import tpu as pltpu
from jax.sharding import Mesh, PartitionSpec as P

Y, X, CORE, Z = 8, 4, 2, 8
LANES = 128
SWAP = ((0, 1), (1, 0))
UP = tuple((i, (i + 1) % X) for i in range(X))
DOWN = tuple((i, (i - 1) % X) for i in range(X))
VMEM = pl.BlockSpec(memory_space=pltpu.VMEM)
SMEM = pl.BlockSpec(memory_space=pltpu.SMEM)
ANY = pl.BlockSpec(memory_space=pl.ANY)
PARTS = 4
GRANT = 32 * 1024 * 1024


def pick_kernel(kept_ref, amplitudes_ref, out_ref, held, sems):
    tiles, keep = kept_ref.shape
    rows = amplitudes_ref.shape[0]
    repeat = Y // tiles
    copies = []
    for a in range(tiles):
        for k in range(keep):
            tile = kept_ref[a, k]
            for r in range(rows):
                held[a, :, r * keep + k] = amplitudes_ref[r, tile]
        for i in range(repeat):
            y = a * repeat + i
            copies.append(pltpu.make_async_copy(held.at[a], out_ref.at[y], sems.at[y]))
            copies[-1].start()
    for copy in copies:
        copy.wait()


def pick(kept_tiles, amplitudes):
    rows, tiles, width = amplitudes.shape
    keep = kept_tiles.shape[1]
    split = amplitudes.reshape(rows, tiles, Z, width // Z // LANES, LANES)
    shape = (Z, rows * keep, width // Z // LANES, LANES)
    return pl.pallas_call(
        pick_kernel,
        out_shape=jax.ShapeDtypeStruct((Y,) + shape, amplitudes.dtype),
        in_specs=[SMEM, VMEM],
        out_specs=ANY,
        scratch_shapes=[
            pltpu.VMEM((kept_tiles.shape[0],) + shape, amplitudes.dtype),
            pltpu.SemaphoreType.DMA((Y,)),
        ],
        cost_estimate=pl.CostEstimate(flops=10**11, bytes_accessed=10**6, transcendentals=0),
        compiler_params=pltpu.CompilerParams(vmem_limit_bytes=GRANT),
    )(kept_tiles, split)


def call(kernel, out_shape, scalars, arrays, work, far=(), scratch=()):
    return pl.pallas_call(
        kernel,
        out_shape=out_shape,
        in_specs=[SMEM] * len(scalars) + [VMEM] * len(arrays) + [ANY] * len(far),
        out_specs=VMEM,
        scratch_shapes=list(scratch),
        cost_estimate=pl.CostEstimate(flops=work, bytes_accessed=1000, transcendentals=0),
        compiler_params=pltpu.CompilerParams(vmem_limit_bytes=GRANT),
    )(*scalars, *arrays, *far)


def low_kernel(in_ref, out_ref):
    out_ref[...] = in_ref[:, :out_ref.shape[1]]


def high_kernel(in_ref, out_ref):
    out_ref[...] = in_ref[:, out_ref.shape[1]:]


def join_kernel(low_ref, high_ref, out_ref):
    half = low_ref.shape[1]
    out_ref[:, :half] = low_ref[...]
    out_ref[:, half:] = high_ref[...]


def rows_kernel(in_ref, out_ref, held, sems):
    rows, keep, peers, _ = out_ref.shape
    chunks, lanes = in_ref.shape[2:]
    part = peers // PARTS
    spans = [pl.ds(p * part, part) for p in range(PARTS)]
    copies = [pltpu.make_async_copy(in_ref.at[span], held.at[span], sems.at[p]) for p, span in enumerate(spans)]
    for copy in copies:
        copy.start()
    for p, copy in enumerate(copies):
        copy.wait()
        low = p * part
        for r in range(rows):
            for k in range(keep):
                for c in range(chunks):
                    at = slice(c * lanes, (c + 1) * lanes)
                    out_ref[r, k, low:low + part, at] = held[low:low + part, r * keep + k, c]


def dots(left_ref, right):
    rows, keep, peers, share = left_ref.shape
    total = None
    for k in range(keep):
        part = lax.dot_general(
            left_ref[:, k].reshape(rows * peers, share),
            right(k),
            (((1,), (1,)), ((), ())),
            preferred_element_type=jnp.float32,
        )
        total = part if total is None else total + part
    return total.astype(jnp.bfloat16).reshape(rows, peers, -1)


def near_kernel(left_ref, own_ref, below_ref, above_ref, out_ref, held, sems):
    keep, block, _ = own_ref.shape
    copies = [pltpu.make_async_copy(above_ref.at[k], held.at[k], sems.at[k]) for k in range(keep)]
    for copy in copies:
        copy.start()
    for j, ref in enumerate((own_ref, below_ref, held)):
        if ref is held:
            for copy in copies:
                copy.wait()
        out_ref[:, :, j * block:(j + 1) * block] = dots(left_ref, lambda k: ref[k])


def far_kernel(core_ref, _, mine_ref, theirs_ref, far_ref, near_mine, near_theirs, out_ref):
    low = near_mine.shape[2]
    for side, (left_ref, near_ref) in enumerate(((mine_ref, near_mine), (theirs_ref, near_theirs))):
        owner = lax.rem(core_ref[0] + side, CORE)
        out_ref[owner, :, :, low:] = dots(left_ref, lambda k: far_ref[k])
        out_ref[owner, :, :, :low] = near_ref[...]


def place_kernel(x_ref, residual_ref, ladder_ref, out_ref):
    groups, cores, _, columns = ladder_ref.shape
    block = columns // X
    for core in range(cores):
        for low, step in enumerate((0, X - 1, 1, 2)):
            at = (lax.rem(x_ref[0] + step, X) * cores + core) * block
            for y in range(groups):
                place = pl.ds(pl.multiple_of(y * X * cores * block + at, block), block)
                ladder = ladder_ref[y, core, :, low * block:(low + 1) * block].astype(jnp.float32)
                total = residual_ref[:, place].astype(jnp.float32) + ladder
                out_ref[:, place] = total.astype(out_ref.dtype)


def shards(amplitudes, integrals, residual_in, kept_tiles):
    rows, tiles, width = amplitudes.shape
    keep = kept_tiles.shape[1]
    share = width // Z
    block = integrals.shape[1]
    x = lax.axis_index("x")
    core = lax.axis_index("c")

    below = lax.ppermute(integrals, "x", UP)
    above = lax.ppermute(integrals, "x", DOWN)
    cut = jax.ShapeDtypeStruct((keep, block // 2, share), integrals.dtype)
    far_low = lax.ppermute(call(low_kernel, cut, (), (below,), 10**11), "x", UP)
    far_high = lax.ppermute(call(high_kernel, cut, (), (above,), 10**11), "x", DOWN)

    outgoing = pick(kept_tiles, amplitudes)
    outgoing = outgoing.reshape(Y * Z, rows * keep, share // LANES, LANES)
    mine = lax.all_to_all(outgoing, ("y", "z"), split_axis=0, concat_axis=0, tiled=True)
    left = jax.ShapeDtypeStruct((rows, keep, Y * Z, share), mine.dtype)
    held = pltpu.VMEM(mine.shape, mine.dtype)
    mine = call(rows_kernel, left, (), (), 1000, (mine,), (held, pltpu.SemaphoreType.DMA((PARTS,))))
    theirs = lax.ppermute(mine, "c", SWAP)

    near_shape = jax.ShapeDtypeStruct((rows, Y * Z, 3 * block), jnp.bfloat16)
    all_shape = jax.ShapeDtypeStruct((CORE, rows, Y * Z, X * block), jnp.bfloat16)
    held = jax.ShapeDtypeStruct(integrals.shape, integrals.dtype)
    room = (pltpu.VMEM(integrals.shape, integrals.dtype), pltpu.SemaphoreType.DMA((keep,)))
    near = [
        call(near_kernel, near_shape, (), (left, integrals, below), 1000, (above,), room)
        for left in (mine, theirs)
    ]
    far = call(join_kernel, held, (), (far_low, far_high), 10**11)
    where = x.astype(jnp.int32).reshape(1)
    which = core.astype(jnp.int32).reshape(1)
    partial = call(far_kernel, all_shape, (which, where), (mine, theirs, far, *near), 1000)
    partial = partial.reshape(CORE, rows, Y, Z, 2, X * block // 2).transpose(2, 0, 3, 1, 4, 5)
    partial = partial.reshape(Y * CORE * Z, rows, 2, X * block // 2)
    returned = lax.all_to_all(partial, ("y", "c", "z"), split_axis=0, concat_axis=0, tiled=True)
    returned = returned.reshape(Y, CORE, Z, rows, 2, X * block // 2).astype(jnp.float32)
    ladder = jnp.sum(returned, axis=2).astype(jnp.bfloat16).reshape(Y, CORE, rows, X * block)
    out = jax.ShapeDtypeStruct(residual_in.shape, residual_in.dtype)
    return call(place_kernel, out, (where,), (residual_in, ladder), 1000)


def solution(mesh):
    fine = Mesh(mesh.devices.reshape(Y, X, CORE, Z), ("y", "x", "c", "z"))
    owner = ("y", "x", "c", "z")
    in_specs = (
        P(owner, None, None),
        P(None, ("y", "x", "c"), "z"),
        P(owner, None),
        P(),
    )
    return jax.shard_map(
        shards, mesh=fine, in_specs=in_specs, out_specs=P(owner, None), check_vma=False
    )
```

```python
import jax
import jax.numpy as jnp
from jax import lax
from jax.experimental import pallas as pl
from jax.experimental.pallas import tpu as pltpu
from jax.sharding import Mesh, PartitionSpec as P

Y, X, CORE, Z = 8, 4, 2, 8
LANES = 128
SWAP = ((0, 1), (1, 0))
SAME = tuple((2 * i + c, 2 * ((i + 1 - 2 * c) % X) + c) for i in range(X) for c in range(CORE))
CROSS = tuple((2 * i + 1 - c, 2 * ((i + 1 - 2 * c) % X) + c) for i in range(X) for c in range(CORE))
HELD = (((0, 0), (X - 1, 0), (X - 1, 1), (2, 0)), ((0, 1), (1, 1), (1, 0), (2, 1)))
VMEM = pl.BlockSpec(memory_space=pltpu.VMEM)
SMEM = pl.BlockSpec(memory_space=pltpu.SMEM)
ANY = pl.BlockSpec(memory_space=pl.ANY)
GRANT = 32 * 1024 * 1024


def pick_kernel(kept_ref, amplitudes_ref, out_ref, held, sems):
    tiles, keep = kept_ref.shape
    rows = amplitudes_ref.shape[0]
    repeat = Y // tiles
    copies = []
    for a in range(tiles):
        for k in range(keep):
            tile = kept_ref[a, k]
            for r in range(rows):
                held[a, :, r * keep + k] = amplitudes_ref[r, tile]
        for i in range(repeat):
            y = a * repeat + i
            copies.append(pltpu.make_async_copy(held.at[a], out_ref.at[y], sems.at[y]))
            copies[-1].start()
    for copy in copies:
        copy.wait()


def pick(kept_tiles, amplitudes):
    rows, tiles, width = amplitudes.shape
    keep = kept_tiles.shape[1]
    split = amplitudes.reshape(rows, tiles, Z, width // Z // LANES, LANES)
    shape = (Z, rows * keep, width // Z // LANES, LANES)
    return pl.pallas_call(
        pick_kernel,
        out_shape=jax.ShapeDtypeStruct((Y,) + shape, amplitudes.dtype),
        in_specs=[SMEM, VMEM],
        out_specs=ANY,
        scratch_shapes=[
            pltpu.VMEM((kept_tiles.shape[0],) + shape, amplitudes.dtype),
            pltpu.SemaphoreType.DMA((Y,)),
        ],
        cost_estimate=pl.CostEstimate(flops=10**11, bytes_accessed=10**6, transcendentals=0),
        compiler_params=pltpu.CompilerParams(vmem_limit_bytes=GRANT),
    )(kept_tiles, split)


def call(kernel, out_shape, scalars, arrays, work, far=(), scratch=()):
    return pl.pallas_call(
        kernel,
        out_shape=out_shape,
        in_specs=[SMEM] * len(scalars) + [VMEM] * len(arrays) + [ANY] * len(far),
        out_specs=(VMEM,) * len(out_shape) if isinstance(out_shape, tuple) else VMEM,
        scratch_shapes=list(scratch),
        cost_estimate=pl.CostEstimate(flops=work, bytes_accessed=1000, transcendentals=0),
        compiler_params=pltpu.CompilerParams(vmem_limit_bytes=GRANT),
    )(*scalars, *arrays, *far)


def hold_kernel(a_ref, b_ref, a_out, b_out):
    pass


def in_place(kernel, arrays, kept, scratch):
    shapes = tuple(jax.ShapeDtypeStruct(a.shape, a.dtype) for a in arrays)
    return pl.pallas_call(
        kernel,
        out_shape=shapes,
        in_specs=[ANY] * len(arrays),
        out_specs=(ANY,) * len(arrays),
        scratch_shapes=scratch,
        input_output_aliases={i: i for i in range(kept)},
        cost_estimate=pl.CostEstimate(flops=10**11, bytes_accessed=10**6, transcendentals=0),
        compiler_params=pltpu.CompilerParams(vmem_limit_bytes=GRANT),
    )(*arrays)


def rows_kernel(in_ref, out_ref):
    rows, keep, _, _ = out_ref.shape
    chunks, lanes = in_ref.shape[2:]
    for r in range(rows):
        for k in range(keep):
            for c in range(chunks):
                out_ref[r, k, :, c * lanes:(c + 1) * lanes] = in_ref[:, r * keep + k, c]


def dots(left_ref, right_ref):
    rows, keep, peers, share = left_ref.shape
    total = None
    for k in range(keep):
        part = lax.dot_general(
            left_ref[:, k].reshape(rows * peers, share),
            right_ref[k],
            (((1,), (1,)), ((), ())),
            preferred_element_type=jnp.float32,
        )
        total = part if total is None else total + part
    return total.astype(jnp.bfloat16).reshape(rows, peers, -1)


def near_kernel(left_ref, *refs):
    rights, out_ref = refs[:-1], refs[-1]
    block = rights[0].shape[1]
    for j, right_ref in enumerate(rights):
        out_ref[:, :, j * block:(j + 1) * block] = dots(left_ref, right_ref)


def rest_kernel(core_ref, _, mine_ref, theirs_ref, near_mine, near_theirs, residual_ref, right_ref, *refs):
    out_ref, residual_out, held, sems = refs
    keep = right_ref.shape[0]
    low = near_mine.shape[2]
    copies = [pltpu.make_async_copy(right_ref.at[k], held.at[k], sems.at[k]) for k in range(keep)]
    for copy in copies:
        copy.start()
    extra = pltpu.make_async_copy(residual_ref, residual_out, sems.at[keep])
    extra.start()
    owners = [lax.rem(core_ref[0] + side, CORE) for side in range(CORE)]
    for owner, near_ref in zip(owners, (near_mine, near_theirs)):
        out_ref[owner, :, :, :low] = near_ref[...]
    for copy in copies:
        copy.wait()
    for owner, left_ref in zip(owners, (mine_ref, theirs_ref)):
        out_ref[owner, :, :, low:] = dots(left_ref, held)
    extra.wait()


def place_kernel(x_ref, residual_ref, ladder_ref, out_ref):
    groups, cores, _, columns = ladder_ref.shape
    block = columns // X
    for core in range(cores):
        for low, (step, side) in enumerate(HELD[core]):
            at = (lax.rem(x_ref[0] + step, X) * cores + side) * block
            for y in range(groups):
                place = pl.ds(pl.multiple_of(y * X * cores * block + at, block), block)
                ladder = ladder_ref[y, core, :, low * block:(low + 1) * block].astype(jnp.float32)
                total = residual_ref[:, place].astype(jnp.float32) + ladder
                out_ref[:, place] = total.astype(out_ref.dtype)


def shards(amplitudes, integrals, residual_in, kept_tiles):
    rows, tiles, width = amplitudes.shape
    keep = kept_tiles.shape[1]
    share = width // Z
    block = integrals.shape[1]
    x = lax.axis_index("x")
    core = lax.axis_index("c")

    first = lax.ppermute(integrals, ("x", "c"), SAME)
    second = lax.ppermute(integrals, ("x", "c"), CROSS)
    first, second = in_place(hold_kernel, (first, second), 2, [])
    third = lax.ppermute(first, ("x", "c"), SAME)

    outgoing = pick(kept_tiles, amplitudes)
    outgoing = outgoing.reshape(Y * Z, rows * keep, share // LANES, LANES)
    mine = lax.all_to_all(outgoing, ("y", "z"), split_axis=0, concat_axis=0, tiled=True)
    left = jax.ShapeDtypeStruct((rows, keep, Y * Z, share), mine.dtype)
    mine = call(rows_kernel, left, (), (mine,), 1000)
    theirs = lax.ppermute(mine, "c", SWAP)

    all_shape = jax.ShapeDtypeStruct((CORE, rows, Y * Z, X * block), jnp.bfloat16)
    near_shape = jax.ShapeDtypeStruct((rows, Y * Z, 3 * block), jnp.bfloat16)
    near = [call(near_kernel, near_shape, (), (a, integrals, first, second), 1000) for a in (mine, theirs)]
    where = x.astype(jnp.int32).reshape(1)
    which = core.astype(jnp.int32).reshape(1)
    out = jax.ShapeDtypeStruct(residual_in.shape, residual_in.dtype)
    room = (pltpu.VMEM(third.shape, third.dtype), pltpu.SemaphoreType.DMA((keep + 1,)))
    partial, residual = call(
        rest_kernel, (all_shape, out), (which, where), (mine, theirs, *near), 1000, (residual_in, third), room
    )
    partial = partial.reshape(CORE, rows, Y, Z, 2, X * block // 2).transpose(2, 0, 3, 1, 4, 5)
    partial = partial.reshape(Y * CORE * Z, rows, 2, X * block // 2)
    returned = lax.all_to_all(partial, ("y", "c", "z"), split_axis=0, concat_axis=0, tiled=True)
    returned = returned.reshape(Y, CORE, Z, rows, 2, X * block // 2).astype(jnp.float32)
    ladder = jnp.sum(returned, axis=2).astype(jnp.bfloat16).reshape(Y, CORE, rows, X * block)
    return call(place_kernel, out, (where,), (residual, ladder), 1000)


def solution(mesh):
    fine = Mesh(mesh.devices.reshape(Y, X, CORE, Z), ("y", "x", "c", "z"))
    owner = ("y", "x", "c", "z")
    in_specs = (
        P(owner, None, None),
        P(None, ("y", "x", "c"), "z"),
        P(owner, None),
        P(),
    )
    return jax.shard_map(
        shards, mesh=fine, in_specs=in_specs, out_specs=P(owner, None), check_vma=False
    )
```

```python
import jax
import jax.numpy as jnp
from jax import lax
from jax.experimental import pallas as pl
from jax.experimental.pallas import tpu as pltpu
from jax.sharding import Mesh, PartitionSpec as P

Y, X, CORE, Z = 8, 4, 2, 8
LANES = 128
SWAP = ((0, 1), (1, 0))
SAME = tuple((2 * i + c, 2 * ((i + 1 - 2 * c) % X) + c) for i in range(X) for c in range(CORE))
CROSS = tuple((2 * i + 1 - c, 2 * ((i + 1 - 2 * c) % X) + c) for i in range(X) for c in range(CORE))
HELD = (((0, 0), (X - 1, 0), (X - 1, 1), (2, 0)), ((0, 1), (1, 1), (1, 0), (2, 1)))
VMEM = pl.BlockSpec(memory_space=pltpu.VMEM)
SMEM = pl.BlockSpec(memory_space=pltpu.SMEM)
ANY = pl.BlockSpec(memory_space=pl.ANY)
GRANT = 32 * 1024 * 1024


def pick_kernel(kept_ref, amplitudes_ref, out_ref, held, sems):
    tiles, keep = kept_ref.shape
    rows = amplitudes_ref.shape[0]
    repeat = Y // tiles
    copies = []
    for a in range(tiles):
        for k in range(keep):
            tile = kept_ref[a, k]
            for r in range(rows):
                held[a, :, r * keep + k] = amplitudes_ref[r, tile]
        for i in range(repeat):
            y = a * repeat + i
            copies.append(pltpu.make_async_copy(held.at[a], out_ref.at[y], sems.at[y]))
            copies[-1].start()
    for copy in copies:
        copy.wait()


def pick(kept_tiles, amplitudes):
    rows, tiles, width = amplitudes.shape
    keep = kept_tiles.shape[1]
    split = amplitudes.reshape(rows, tiles, Z, width // Z // LANES, LANES)
    shape = (Z, rows * keep, width // Z // LANES, LANES)
    return pl.pallas_call(
        pick_kernel,
        out_shape=jax.ShapeDtypeStruct((Y,) + shape, amplitudes.dtype),
        in_specs=[SMEM, VMEM],
        out_specs=ANY,
        scratch_shapes=[
            pltpu.VMEM((kept_tiles.shape[0],) + shape, amplitudes.dtype),
            pltpu.SemaphoreType.DMA((Y,)),
        ],
        cost_estimate=pl.CostEstimate(flops=10**11, bytes_accessed=10**6, transcendentals=0),
        compiler_params=pltpu.CompilerParams(vmem_limit_bytes=GRANT),
    )(kept_tiles, split)


def call(kernel, out_shape, scalars, arrays, work, far=(), scratch=()):
    return pl.pallas_call(
        kernel,
        out_shape=out_shape,
        in_specs=[SMEM] * len(scalars) + [VMEM] * len(arrays) + [ANY] * len(far),
        out_specs=(VMEM,) * len(out_shape) if isinstance(out_shape, tuple) else VMEM,
        scratch_shapes=list(scratch),
        cost_estimate=pl.CostEstimate(flops=work, bytes_accessed=1000, transcendentals=0),
        compiler_params=pltpu.CompilerParams(vmem_limit_bytes=GRANT),
    )(*scalars, *arrays, *far)


def hold_kernel(a_ref, b_ref, a_out, b_out):
    pass


def in_place(kernel, arrays, kept, scratch):
    shapes = tuple(jax.ShapeDtypeStruct(a.shape, a.dtype) for a in arrays)
    return pl.pallas_call(
        kernel,
        out_shape=shapes,
        in_specs=[ANY] * len(arrays),
        out_specs=(ANY,) * len(arrays),
        scratch_shapes=scratch,
        input_output_aliases={i: i for i in range(kept)},
        cost_estimate=pl.CostEstimate(flops=10**11, bytes_accessed=10**6, transcendentals=0),
        compiler_params=pltpu.CompilerParams(vmem_limit_bytes=GRANT),
    )(*arrays)


def arrange(in_ref, wide, left_ref):
    rows, keep, peers, share = left_ref.shape
    chunks = share // LANES
    wide[...] = in_ref[...].astype(jnp.float32)
    for r in range(rows):
        for k in range(keep):
            for c in range(chunks):
                at = pl.ds((r * keep + k) * chunks + c, peers, rows * keep * chunks)
                left_ref[r, k, :, c * LANES:(c + 1) * LANES] = wide[at, :].astype(left_ref.dtype)


def dots(left_ref, right_ref):
    rows, keep, peers, share = left_ref.shape
    total = None
    for k in range(keep):
        part = lax.dot_general(
            left_ref[:, k].reshape(rows * peers, share),
            right_ref[k],
            (((1,), (1,)), ((), ())),
            preferred_element_type=jnp.float32,
        )
        total = part if total is None else total + part
    return total


def near_kernel(in_ref, *refs):
    rights, (left_ref, out_ref, wide) = refs[:-3], refs[-3:]
    block = rights[0].shape[1]
    arrange(in_ref, wide, left_ref)
    for j, right_ref in enumerate(rights):
        out_ref[:, j * block:(j + 1) * block] = dots(left_ref, right_ref)


def rest_kernel(core_ref, _, mine_ref, near_ref, in_ref, *refs):
    rights = refs[:-9]
    residual_ref, third_ref, out_ref, residual_out, theirs_ref, held, wide, strips, sems = refs[-9:]
    rows, keep, _, _ = mine_ref.shape
    block = third_ref.shape[1]
    chunks = X * block // LANES
    copies = [pltpu.make_async_copy(third_ref.at[k], held.at[k], sems.at[k]) for k in range(keep)]
    for copy in copies:
        copy.start()
    extra = pltpu.make_async_copy(residual_ref, residual_out, sems.at[keep])
    extra.start()

    def put(side, low, values):
        for r in range(rows):
            for y in range(Y):
                for c in range(values.shape[1] // LANES):
                    start = ((side * Y + y) * Z * rows + r) * chunks + low // LANES + c
                    piece = values[(r * Y + y) * Z:(r * Y + y + 1) * Z, c * LANES:(c + 1) * LANES]
                    strips[pl.ds(start, Z, rows * chunks), :] = piece

    arrange(in_ref, wide, theirs_ref)
    put(0, 0, near_ref[...])
    for j, right_ref in enumerate(rights):
        put(1, j * block, dots(theirs_ref, right_ref))
    for copy in copies:
        copy.wait()
    for side, left_ref in enumerate((mine_ref, theirs_ref)):
        put(side, len(rights) * block, dots(left_ref, held))
        owner = lax.rem(core_ref[0] + side, CORE)
        size = Z * rows * chunks
        for y in range(Y):
            start = (side * Y + y) * size
            out_ref[y, owner] = strips[start:start + size, :].astype(out_ref.dtype)
    extra.wait()


def place_kernel(x_ref, residual_ref, ladder_ref, out_ref):
    groups, cores, _, columns = ladder_ref.shape
    block = columns // X
    for core in range(cores):
        for low, (step, side) in enumerate(HELD[core]):
            at = (lax.rem(x_ref[0] + step, X) * cores + side) * block
            for y in range(groups):
                place = pl.ds(pl.multiple_of(y * X * cores * block + at, block), block)
                ladder = ladder_ref[y, core, :, low * block:(low + 1) * block].astype(jnp.float32)
                total = residual_ref[:, place].astype(jnp.float32) + ladder
                out_ref[:, place] = total.astype(out_ref.dtype)


def shards(amplitudes, integrals, residual_in, kept_tiles):
    rows, tiles, width = amplitudes.shape
    keep = kept_tiles.shape[1]
    share = width // Z
    block = integrals.shape[1]
    x = lax.axis_index("x")
    core = lax.axis_index("c")

    first = lax.ppermute(integrals, ("x", "c"), SAME)
    second = lax.ppermute(integrals, ("x", "c"), CROSS)
    first, second = in_place(hold_kernel, (first, second), 2, [])
    third = lax.ppermute(first, ("x", "c"), SAME)

    outgoing = pick(kept_tiles, amplitudes)
    outgoing = outgoing.reshape(Y * Z, rows * keep, share // LANES, LANES)
    mine = lax.all_to_all(outgoing, ("y", "z"), split_axis=0, concat_axis=0, tiled=True)
    left = jax.ShapeDtypeStruct((rows, keep, Y * Z, share), mine.dtype)
    theirs = lax.ppermute(mine, "c", SWAP)

    chunks = X * block // LANES
    all_shape = jax.ShapeDtypeStruct((Y, CORE, Z * rows * chunks, LANES), jnp.bfloat16)
    mine = mine.reshape(-1, LANES)
    wide = pltpu.VMEM(mine.shape, jnp.float32)
    near_shape = jax.ShapeDtypeStruct((rows * Y * Z, 3 * block), jnp.float32)
    near_blocks = (integrals, first, second)
    mine, near = call(near_kernel, (left, near_shape), (), (mine, *near_blocks), 1000, (), (wide,))
    where = x.astype(jnp.int32).reshape(1)
    which = core.astype(jnp.int32).reshape(1)
    out = jax.ShapeDtypeStruct(residual_in.shape, residual_in.dtype)
    room = (
        pltpu.VMEM(left.shape, left.dtype),
        pltpu.VMEM(third.shape, third.dtype),
        wide,
        pltpu.VMEM((CORE * Y * Z * rows * chunks, LANES), jnp.float32),
        pltpu.SemaphoreType.DMA((keep + 1,)),
    )
    partial, residual = call(
        rest_kernel,
        (all_shape, out),
        (which, where),
        (mine, near, theirs.reshape(-1, LANES), *near_blocks),
        1000,
        (residual_in, third),
        room,
    )
    partial = partial.reshape(Y * CORE * Z, rows * chunks, LANES)
    returned = lax.all_to_all(partial, ("y", "c", "z"), split_axis=0, concat_axis=0, tiled=True)
    returned = returned.reshape(Y, CORE, Z, rows * chunks, LANES).astype(jnp.float32)
    ladder = jnp.sum(returned, axis=2).astype(jnp.bfloat16).reshape(Y, CORE, rows, X * block)
    return call(place_kernel, out, (where,), (residual, ladder), 1000)


def solution(mesh):
    fine = Mesh(mesh.devices.reshape(Y, X, CORE, Z), ("y", "x", "c", "z"))
    owner = ("y", "x", "c", "z")
    in_specs = (
        P(owner, None, None),
        P(None, ("y", "x", "c"), "z"),
        P(owner, None),
        P(),
    )
    return jax.shard_map(
        shards, mesh=fine, in_specs=in_specs, out_specs=P(owner, None), check_vma=False
    )
```

```python
import jax
import jax.numpy as jnp
from jax import lax
from jax.experimental import pallas as pl
from jax.experimental.pallas import tpu as pltpu
from jax.sharding import Mesh, PartitionSpec as P

Y, X, CORE, Z = 8, 4, 2, 8
LANES = 128
SWAP = ((0, 1), (1, 0))
SAME = tuple((2 * i + c, 2 * ((i + 1 - 2 * c) % X) + c) for i in range(X) for c in range(CORE))
CROSS = tuple((2 * i + 1 - c, 2 * ((i + 1 - 2 * c) % X) + c) for i in range(X) for c in range(CORE))
HELD = (((0, 0), (X - 1, 0), (X - 1, 1), (2, 0)), ((0, 1), (1, 1), (1, 0), (2, 1)))
VMEM = pl.BlockSpec(memory_space=pltpu.VMEM)
SMEM = pl.BlockSpec(memory_space=pltpu.SMEM)
ANY = pl.BlockSpec(memory_space=pl.ANY)
GRANT = 32 * 1024 * 1024


def pick_kernel(kept_ref, amplitudes_ref, out_ref, held, sems):
    tiles, keep = kept_ref.shape
    rows = amplitudes_ref.shape[0]
    repeat = Y // tiles
    copies = []
    for a in range(tiles):
        for k in range(keep):
            tile = kept_ref[a, k]
            for r in range(rows):
                held[a, :, r * keep + k] = amplitudes_ref[r, tile]
        for i in range(repeat):
            y = a * repeat + i
            copies.append(pltpu.make_async_copy(held.at[a], out_ref.at[y], sems.at[y]))
            copies[-1].start()
    for copy in copies:
        copy.wait()


def pick(kept_tiles, amplitudes):
    rows, tiles, width = amplitudes.shape
    keep = kept_tiles.shape[1]
    split = amplitudes.reshape(rows, tiles, Z, width // Z // LANES, LANES)
    shape = (Z, rows * keep, width // Z // LANES, LANES)
    return pl.pallas_call(
        pick_kernel,
        out_shape=jax.ShapeDtypeStruct((Y,) + shape, amplitudes.dtype),
        in_specs=[SMEM, VMEM],
        out_specs=ANY,
        scratch_shapes=[
            pltpu.VMEM((kept_tiles.shape[0],) + shape, amplitudes.dtype),
            pltpu.SemaphoreType.DMA((Y,)),
        ],
        cost_estimate=pl.CostEstimate(flops=10**11, bytes_accessed=10**6, transcendentals=0),
        compiler_params=pltpu.CompilerParams(vmem_limit_bytes=GRANT),
    )(kept_tiles, split)


def call(kernel, out_shape, scalars, arrays, work, far=(), scratch=()):
    return pl.pallas_call(
        kernel,
        out_shape=out_shape,
        in_specs=[SMEM] * len(scalars) + [VMEM] * len(arrays) + [ANY] * len(far),
        out_specs=(VMEM,) * len(out_shape) if isinstance(out_shape, tuple) else VMEM,
        scratch_shapes=list(scratch),
        cost_estimate=pl.CostEstimate(flops=work, bytes_accessed=1000, transcendentals=0),
        compiler_params=pltpu.CompilerParams(vmem_limit_bytes=GRANT),
    )(*scalars, *arrays, *far)


def hold_kernel(a_ref, b_ref, a_out, b_out):
    pass


def in_place(kernel, arrays, kept, scratch):
    shapes = tuple(jax.ShapeDtypeStruct(a.shape, a.dtype) for a in arrays)
    return pl.pallas_call(
        kernel,
        out_shape=shapes,
        in_specs=[ANY] * len(arrays),
        out_specs=(ANY,) * len(arrays),
        scratch_shapes=scratch,
        input_output_aliases={i: i for i in range(kept)},
        cost_estimate=pl.CostEstimate(flops=10**11, bytes_accessed=10**6, transcendentals=0),
        compiler_params=pltpu.CompilerParams(vmem_limit_bytes=GRANT),
    )(*arrays)


def arrange(in_ref, wide, left_ref):
    rows, keep, peers, share = left_ref.shape
    chunks = share // LANES
    wide[...] = in_ref[...].astype(jnp.float32)
    for r in range(rows):
        for k in range(keep):
            for c in range(chunks):
                at = pl.ds((r * keep + k) * chunks + c, peers, rows * keep * chunks)
                left_ref[r, k, :, c * LANES:(c + 1) * LANES] = wide[at, :].astype(left_ref.dtype)


def dots(left_ref, right_ref):
    rows, keep, peers, share = left_ref.shape
    total = None
    for k in range(keep):
        part = lax.dot_general(
            left_ref[:, k].reshape(rows * peers, share),
            right_ref[k],
            (((1,), (1,)), ((), ())),
            preferred_element_type=jnp.float32,
        )
        total = part if total is None else total + part
    return total


def near_kernel(in_ref, *refs):
    rights, (left_ref, out_ref, wide) = refs[:-3], refs[-3:]
    block = rights[0].shape[1]
    arrange(in_ref, wide, left_ref)
    for j, right_ref in enumerate(rights):
        out_ref[:, j * block:(j + 1) * block] = dots(left_ref, right_ref)


def rest_kernel(core_ref, _, mine_ref, near_ref, in_ref, *refs):
    rights = refs[:-9]
    residual_ref, third_ref, out_ref, residual_out, theirs_ref, held, wide, strips, sems = refs[-9:]
    rows, keep, _, _ = mine_ref.shape
    block = third_ref.shape[1]
    chunks = X * block // LANES
    copies = [pltpu.make_async_copy(third_ref.at[k], held.at[k], sems.at[k]) for k in range(keep)]
    for copy in copies:
        copy.start()
    extra = pltpu.make_async_copy(residual_ref, residual_out, sems.at[keep])
    extra.start()

    def put(side, low, values):
        for r in range(rows):
            for y in range(Y):
                for c in range(values.shape[1] // LANES):
                    start = ((side * Y + y) * Z * rows + r) * chunks + low // LANES + c
                    piece = values[(r * Y + y) * Z:(r * Y + y + 1) * Z, c * LANES:(c + 1) * LANES]
                    strips[pl.ds(start, Z, rows * chunks), :] = piece

    arrange(in_ref, wide, theirs_ref)
    put(0, 0, near_ref[...])
    for j, right_ref in enumerate(rights):
        put(1, j * block, dots(theirs_ref, right_ref))
    for copy in copies:
        copy.wait()
    for side, left_ref in enumerate((mine_ref, theirs_ref)):
        put(side, len(rights) * block, dots(left_ref, held))
        owner = lax.rem(core_ref[0] + side, CORE)
        size = Z * rows * chunks
        for y in range(Y):
            start = (side * Y + y) * size
            piece = strips[start:start + size, :].astype(out_ref.dtype)
            out_ref[y, :, owner] = piece.reshape(Z, rows * chunks, LANES)
    extra.wait()


def place_kernel(x_ref, residual_ref, ladder_ref, out_ref):
    groups, cores, _, columns = ladder_ref.shape
    block = columns // X
    for core in range(cores):
        for low, (step, side) in enumerate(HELD[core]):
            at = (lax.rem(x_ref[0] + step, X) * cores + side) * block
            for y in range(groups):
                place = pl.ds(pl.multiple_of(y * X * cores * block + at, block), block)
                ladder = ladder_ref[y, core, :, low * block:(low + 1) * block].astype(jnp.float32)
                total = residual_ref[:, place].astype(jnp.float32) + ladder
                out_ref[:, place] = total.astype(out_ref.dtype)


def shards(amplitudes, integrals, residual_in, kept_tiles):
    rows, tiles, width = amplitudes.shape
    keep = kept_tiles.shape[1]
    share = width // Z
    block = integrals.shape[1]
    x = lax.axis_index("x")
    core = lax.axis_index("c")

    first = lax.ppermute(integrals, ("x", "c"), SAME)
    second = lax.ppermute(integrals, ("x", "c"), CROSS)
    first, second = in_place(hold_kernel, (first, second), 2, [])
    third = lax.ppermute(first, ("x", "c"), SAME)

    outgoing = pick(kept_tiles, amplitudes)
    outgoing = outgoing.reshape(Y * Z, rows * keep, share // LANES, LANES)
    mine = lax.all_to_all(outgoing, ("y", "z"), split_axis=0, concat_axis=0, tiled=True)
    left = jax.ShapeDtypeStruct((rows, keep, Y * Z, share), mine.dtype)
    theirs = lax.ppermute(mine, "c", SWAP)

    chunks = X * block // LANES
    all_shape = jax.ShapeDtypeStruct((Y, Z, CORE, rows * chunks, LANES), jnp.bfloat16)
    mine = mine.reshape(-1, LANES)
    wide = pltpu.VMEM(mine.shape, jnp.float32)
    near_shape = jax.ShapeDtypeStruct((rows * Y * Z, 3 * block), jnp.float32)
    near_blocks = (integrals, first, second)
    mine, near = call(near_kernel, (left, near_shape), (), (mine, *near_blocks), 1000, (), (wide,))
    where = x.astype(jnp.int32).reshape(1)
    which = core.astype(jnp.int32).reshape(1)
    out = jax.ShapeDtypeStruct(residual_in.shape, residual_in.dtype)
    room = (
        pltpu.VMEM(left.shape, left.dtype),
        pltpu.VMEM(third.shape, third.dtype),
        wide,
        pltpu.VMEM((CORE * Y * Z * rows * chunks, LANES), jnp.float32),
        pltpu.SemaphoreType.DMA((keep + 1,)),
    )
    partial, residual = call(
        rest_kernel,
        (all_shape, out),
        (which, where),
        (mine, near, theirs.reshape(-1, LANES), *near_blocks),
        1000,
        (residual_in, third),
        room,
    )
    partial = partial.reshape(Y * CORE * Z, rows * chunks, LANES)
    returned = lax.all_to_all(partial, ("y", "z", "c"), split_axis=0, concat_axis=0, tiled=True)
    returned = returned.reshape(Y, Z, CORE, rows * chunks, LANES).astype(jnp.float32)
    ladder = jnp.sum(returned, axis=1).astype(jnp.bfloat16).reshape(Y, CORE, rows, X * block)
    return call(place_kernel, out, (where,), (residual, ladder), 1000)


def solution(mesh):
    fine = Mesh(mesh.devices.reshape(Y, X, CORE, Z), ("y", "x", "c", "z"))
    owner = ("y", "x", "c", "z")
    in_specs = (
        P(owner, None, None),
        P(None, ("y", "x", "c"), "z"),
        P(owner, None),
        P(),
    )
    return jax.shard_map(
        shards, mesh=fine, in_specs=in_specs, out_specs=P(owner, None), check_vma=False
    )
```

```python
import jax
import jax.numpy as jnp
from jax import lax
from jax.experimental import pallas as pl
from jax.experimental.pallas import tpu as pltpu
from jax.sharding import Mesh, PartitionSpec as P

Y, X, CORE, Z = 8, 4, 2, 8
LANES = 128
SWAP = ((0, 1), (1, 0))
SAME = tuple((2 * i + c, 2 * ((i + 1 - 2 * c) % X) + c) for i in range(X) for c in range(CORE))
CROSS = tuple((2 * i + 1 - c, 2 * ((i + 1 - 2 * c) % X) + c) for i in range(X) for c in range(CORE))
HELD = (((0, 0), (X - 1, 0), (X - 1, 1), (2, 0)), ((0, 1), (1, 1), (1, 0), (2, 1)))
AXES = ("y2", "y1", "y0", "x", "c", "z2", "z1", "z0")
GROUP = ("y0", "y1", "y2", "z0", "z1", "z2")
VMEM = pl.BlockSpec(memory_space=pltpu.VMEM)
SMEM = pl.BlockSpec(memory_space=pltpu.SMEM)
ANY = pl.BlockSpec(memory_space=pl.ANY)
GRANT = 32 * 1024 * 1024


def pick_kernel(kept_ref, amplitudes_ref, out_ref, held, sems):
    tiles, keep = kept_ref.shape
    rows = amplitudes_ref.shape[0]
    repeat = Y // tiles
    copies = []
    for a in range(tiles):
        for k in range(keep):
            tile = kept_ref[a, k]
            for r in range(rows):
                held[a, :, :, :, r * keep + k] = amplitudes_ref[r, tile]
        for i in range(repeat):
            y = a * repeat + i
            place = out_ref.at[y % 2, y // 2 % 2, y // 4]
            copies.append(pltpu.make_async_copy(held.at[a], place, sems.at[y]))
            copies[-1].start()
    for copy in copies:
        copy.wait()


def pick(kept_tiles, amplitudes):
    rows, tiles, width = amplitudes.shape
    keep = kept_tiles.shape[1]
    split = amplitudes.reshape(rows, tiles, 2, 2, 2, width // Z // LANES, LANES)
    split = split.transpose(0, 1, 4, 3, 2, 5, 6)
    shape = (Z, rows * keep, width // Z // LANES, LANES)
    return pl.pallas_call(
        pick_kernel,
        out_shape=jax.ShapeDtypeStruct((2,) * 6 + shape[1:], amplitudes.dtype),
        in_specs=[SMEM, VMEM],
        out_specs=ANY,
        scratch_shapes=[
            pltpu.VMEM((kept_tiles.shape[0], 2, 2, 2) + shape[1:], amplitudes.dtype),
            pltpu.SemaphoreType.DMA((Y,)),
        ],
        cost_estimate=pl.CostEstimate(flops=10**11, bytes_accessed=10**6, transcendentals=0),
        compiler_params=pltpu.CompilerParams(vmem_limit_bytes=GRANT),
    )(kept_tiles, split)


def call(kernel, out_shape, scalars, arrays, work, far=(), scratch=()):
    return pl.pallas_call(
        kernel,
        out_shape=out_shape,
        in_specs=[SMEM] * len(scalars) + [VMEM] * len(arrays) + [ANY] * len(far),
        out_specs=(VMEM,) * len(out_shape) if isinstance(out_shape, tuple) else VMEM,
        scratch_shapes=list(scratch),
        cost_estimate=pl.CostEstimate(flops=work, bytes_accessed=1000, transcendentals=0),
        compiler_params=pltpu.CompilerParams(vmem_limit_bytes=GRANT),
    )(*scalars, *arrays, *far)


def hold_kernel(a_ref, b_ref, a_out, b_out):
    pass


def in_place(kernel, arrays, kept, scratch):
    shapes = tuple(jax.ShapeDtypeStruct(a.shape, a.dtype) for a in arrays)
    return pl.pallas_call(
        kernel,
        out_shape=shapes,
        in_specs=[ANY] * len(arrays),
        out_specs=(ANY,) * len(arrays),
        scratch_shapes=scratch,
        input_output_aliases={i: i for i in range(kept)},
        cost_estimate=pl.CostEstimate(flops=10**11, bytes_accessed=10**6, transcendentals=0),
        compiler_params=pltpu.CompilerParams(vmem_limit_bytes=GRANT),
    )(*arrays)


def arrange(in_ref, wide, left_ref):
    rows, keep, peers, share = left_ref.shape
    chunks = share // LANES
    wide[...] = in_ref[...].astype(jnp.float32)
    for r in range(rows):
        for k in range(keep):
            for c in range(chunks):
                at = pl.ds((r * keep + k) * chunks + c, peers, rows * keep * chunks)
                left_ref[r, k, :, c * LANES:(c + 1) * LANES] = wide[at, :].astype(left_ref.dtype)


def dots(left_ref, right_ref):
    rows, keep, peers, share = left_ref.shape
    total = None
    for k in range(keep):
        part = lax.dot_general(
            left_ref[:, k].reshape(rows * peers, share),
            right_ref[k],
            (((1,), (1,)), ((), ())),
            preferred_element_type=jnp.float32,
        )
        total = part if total is None else total + part
    return total


def near_kernel(in_ref, *refs):
    rights, (left_ref, out_ref, wide) = refs[:-3], refs[-3:]
    block = rights[0].shape[1]
    arrange(in_ref, wide, left_ref)
    for j, right_ref in enumerate(rights):
        out_ref[:, j * block:(j + 1) * block] = dots(left_ref, right_ref)


def rest_kernel(core_ref, _, mine_ref, near_ref, in_ref, *refs):
    rights = refs[:-9]
    residual_ref, third_ref, out_ref, residual_out, theirs_ref, held, wide, strips, sems = refs[-9:]
    rows, keep, _, _ = mine_ref.shape
    block = third_ref.shape[1]
    chunks = X * block // LANES
    copies = [pltpu.make_async_copy(third_ref.at[k], held.at[k], sems.at[k]) for k in range(keep)]
    for copy in copies:
        copy.start()
    extra = pltpu.make_async_copy(residual_ref, residual_out, sems.at[keep])
    extra.start()

    def put(side, low, values):
        for r in range(rows):
            for y in range(Y):
                for c in range(values.shape[1] // LANES):
                    start = ((side * Y + y) * Z * rows + r) * chunks + low // LANES + c
                    piece = values[(r * Y + y) * Z:(r * Y + y + 1) * Z, c * LANES:(c + 1) * LANES]
                    strips[pl.ds(start, Z, rows * chunks), :] = piece

    arrange(in_ref, wide, theirs_ref)
    put(0, 0, near_ref[...])
    for j, right_ref in enumerate(rights):
        put(1, j * block, dots(theirs_ref, right_ref))
    for copy in copies:
        copy.wait()
    for side, left_ref in enumerate((mine_ref, theirs_ref)):
        put(side, len(rights) * block, dots(left_ref, held))
        owner = lax.rem(core_ref[0] + side, CORE)
        size = Z * rows * chunks
        for y in range(Y):
            start = (side * Y + y) * size
            piece = strips[start:start + size, :].astype(out_ref.dtype)
            out_ref[y, :, owner] = piece.reshape(Z, rows * chunks, LANES)
    extra.wait()


def place_kernel(x_ref, residual_ref, ladder_ref, out_ref):
    groups, cores, _, columns = ladder_ref.shape
    block = columns // X
    for core in range(cores):
        for low, (step, side) in enumerate(HELD[core]):
            at = (lax.rem(x_ref[0] + step, X) * cores + side) * block
            for y in range(groups):
                place = pl.ds(pl.multiple_of(y * X * cores * block + at, block), block)
                ladder = ladder_ref[y, core, :, low * block:(low + 1) * block].astype(jnp.float32)
                total = residual_ref[:, place].astype(jnp.float32) + ladder
                out_ref[:, place] = total.astype(out_ref.dtype)


def shards(amplitudes, integrals, residual_in, kept_tiles):
    rows, tiles, width = amplitudes.shape
    keep = kept_tiles.shape[1]
    share = width // Z
    block = integrals.shape[1]
    x = lax.axis_index("x")
    core = lax.axis_index("c")

    first = lax.ppermute(integrals, ("x", "c"), SAME)
    second = lax.ppermute(integrals, ("x", "c"), CROSS)
    first, second = in_place(hold_kernel, (first, second), 2, [])
    third = lax.ppermute(first, ("x", "c"), SAME)

    outgoing = pick(kept_tiles, amplitudes)
    outgoing = outgoing.reshape(Y * Z, rows * keep, share // LANES, LANES)
    mine = lax.all_to_all(outgoing, GROUP, split_axis=0, concat_axis=0, tiled=True)
    left = jax.ShapeDtypeStruct((rows, keep, Y * Z, share), mine.dtype)
    theirs = lax.ppermute(mine, "c", SWAP)

    chunks = X * block // LANES
    all_shape = jax.ShapeDtypeStruct((Y, Z, CORE, rows * chunks, LANES), jnp.bfloat16)
    mine = mine.reshape(-1, LANES)
    wide = pltpu.VMEM(mine.shape, jnp.float32)
    near_shape = jax.ShapeDtypeStruct((rows * Y * Z, 3 * block), jnp.float32)
    near_blocks = (integrals, first, second)
    mine, near = call(near_kernel, (left, near_shape), (), (mine, *near_blocks), 1000, (), (wide,))
    where = x.astype(jnp.int32).reshape(1)
    which = core.astype(jnp.int32).reshape(1)
    out = jax.ShapeDtypeStruct(residual_in.shape, residual_in.dtype)
    room = (
        pltpu.VMEM(left.shape, left.dtype),
        pltpu.VMEM(third.shape, third.dtype),
        wide,
        pltpu.VMEM((CORE * Y * Z * rows * chunks, LANES), jnp.float32),
        pltpu.SemaphoreType.DMA((keep + 1,)),
    )
    partial, residual = call(
        rest_kernel,
        (all_shape, out),
        (which, where),
        (mine, near, theirs.reshape(-1, LANES), *near_blocks),
        1000,
        (residual_in, third),
        room,
    )
    partial = partial.reshape(Y * CORE * Z, rows * chunks, LANES)
    returned = lax.all_to_all(partial, GROUP + ("c",), split_axis=0, concat_axis=0, tiled=True)
    returned = returned.reshape((2,) * 6 + (CORE, rows * chunks, LANES)).astype(jnp.float32)
    ladder = jnp.sum(returned, axis=(3, 4, 5)).astype(jnp.bfloat16)
    ladder = ladder.transpose(2, 1, 0, 3, 4, 5).reshape(Y, CORE, rows, X * block)
    return call(place_kernel, out, (where,), (residual, ladder), 1000)


def solution(mesh):
    fine = Mesh(mesh.devices.reshape(2, 2, 2, X, CORE, 2, 2, 2), AXES)
    in_specs = (
        P(AXES, None, None),
        P(None, AXES[:5], AXES[5:]),
        P(AXES, None),
        P(),
    )
    return jax.shard_map(
        shards, mesh=fine, in_specs=in_specs, out_specs=P(AXES, None), check_vma=False
    )
```

```python
import jax
import jax.numpy as jnp
from jax import lax
from jax.experimental import pallas as pl
from jax.experimental.pallas import tpu as pltpu
from jax.sharding import Mesh, PartitionSpec as P

Y, X, CORE, Z = 8, 4, 2, 8
LANES = 128
SWAP = ((0, 1), (1, 0))
SAME = tuple((2 * i + c, 2 * ((i + 1 - 2 * c) % X) + c) for i in range(X) for c in range(CORE))
CROSS = tuple((2 * i + 1 - c, 2 * ((i + 1 - 2 * c) % X) + c) for i in range(X) for c in range(CORE))
HELD = (((0, 0), (X - 1, 0), (X - 1, 1), (2, 0)), ((0, 1), (1, 1), (1, 0), (2, 1)))
AXES = ("y2", "y1", "y0", "x", "c", "z2", "z1", "z0")
GROUP = ("y0", "y1", "y2", "z0", "z1", "z2")
VMEM = pl.BlockSpec(memory_space=pltpu.VMEM)
SMEM = pl.BlockSpec(memory_space=pltpu.SMEM)
ANY = pl.BlockSpec(memory_space=pl.ANY)
GRANT = 32 * 1024 * 1024
SPARE = 64


def pick_kernel(kept_ref, amplitudes_ref, out_ref, held, sems):
    tiles, keep = kept_ref.shape
    rows = amplitudes_ref.shape[0]
    repeat = Y // tiles
    copies = []
    for a in range(tiles):
        for k in range(keep):
            tile = kept_ref[a, k]
            for r in range(rows):
                held[a, :, :, :, r * keep + k] = amplitudes_ref[r, tile]
        for i in range(repeat):
            y = a * repeat + i
            place = out_ref.at[y % 2, y // 2 % 2, y // 4]
            copies.append(pltpu.make_async_copy(held.at[a], place, sems.at[y]))
            copies[-1].start()
    for copy in copies:
        copy.wait()


def pick(kept_tiles, amplitudes):
    rows, tiles, width = amplitudes.shape
    keep = kept_tiles.shape[1]
    split = amplitudes.reshape(rows, tiles, 2, 2, 2, width // Z // LANES, LANES)
    split = split.transpose(0, 1, 4, 3, 2, 5, 6)
    shape = (Z, rows * keep, width // Z // LANES, LANES)
    return pl.pallas_call(
        pick_kernel,
        out_shape=jax.ShapeDtypeStruct((2,) * 6 + shape[1:], amplitudes.dtype),
        in_specs=[SMEM, VMEM],
        out_specs=ANY,
        scratch_shapes=[
            pltpu.VMEM((kept_tiles.shape[0], 2, 2, 2) + shape[1:], amplitudes.dtype),
            pltpu.SemaphoreType.DMA((Y,)),
        ],
        cost_estimate=pl.CostEstimate(flops=10**11, bytes_accessed=10**6, transcendentals=0),
        compiler_params=pltpu.CompilerParams(vmem_limit_bytes=GRANT),
    )(kept_tiles, split)


def call(kernel, out_shape, scalars, arrays, work, far=(), scratch=()):
    return pl.pallas_call(
        kernel,
        out_shape=out_shape,
        in_specs=[SMEM] * len(scalars) + [VMEM] * len(arrays) + [ANY] * len(far),
        out_specs=(VMEM,) * len(out_shape) if isinstance(out_shape, tuple) else VMEM,
        scratch_shapes=list(scratch),
        cost_estimate=pl.CostEstimate(flops=work, bytes_accessed=1000, transcendentals=0),
        compiler_params=pltpu.CompilerParams(vmem_limit_bytes=GRANT),
    )(*scalars, *arrays, *far)


def hold_kernel(a_ref, b_ref, a_out, b_out):
    pass


def in_place(kernel, arrays, kept, scratch):
    shapes = tuple(jax.ShapeDtypeStruct(a.shape, a.dtype) for a in arrays)
    return pl.pallas_call(
        kernel,
        out_shape=shapes,
        in_specs=[ANY] * len(arrays),
        out_specs=(ANY,) * len(arrays),
        scratch_shapes=scratch,
        input_output_aliases={i: i for i in range(kept)},
        cost_estimate=pl.CostEstimate(flops=10**11, bytes_accessed=10**6, transcendentals=0),
        compiler_params=pltpu.CompilerParams(vmem_limit_bytes=GRANT),
    )(*arrays)


def arrange(in_ref, wide, left_ref):
    rows, keep, peers, share = left_ref.shape
    chunks = share // LANES
    wide[:in_ref.shape[0], :] = in_ref[...].astype(jnp.float32)
    for r in range(rows):
        for k in range(keep):
            for c in range(chunks):
                at = pl.ds((r * keep + k) * chunks + c, peers, rows * keep * chunks)
                left_ref[r, k, :, c * LANES:(c + 1) * LANES] = wide[at, :].astype(left_ref.dtype)


def dots(left_ref, right_ref):
    rows, keep, peers, share = left_ref.shape
    total = None
    for k in range(keep):
        part = lax.dot_general(
            left_ref[:, k].reshape(rows * peers, share),
            right_ref[k],
            (((1,), (1,)), ((), ())),
            preferred_element_type=jnp.float32,
        )
        total = part if total is None else total + part
    return total


def near_kernel(in_ref, *refs):
    rights, (left_ref, out_ref, wide) = refs[:-3], refs[-3:]
    block = rights[0].shape[1]
    arrange(in_ref, wide, left_ref)
    for j, right_ref in enumerate(rights):
        out_ref[:, j * block:(j + 1) * block] = dots(left_ref, right_ref)


def rest_kernel(core_ref, _, mine_ref, near_ref, in_ref, *refs):
    rights = refs[:-9]
    residual_ref, third_ref, out_ref, residual_out, theirs_ref, held, wide, strips, sems = refs[-9:]
    rows, keep, _, _ = mine_ref.shape
    block = third_ref.shape[1]
    chunks = X * block // LANES
    copies = [pltpu.make_async_copy(third_ref.at[k], held.at[k], sems.at[k]) for k in range(keep)]
    for copy in copies:
        copy.start()
    extra = pltpu.make_async_copy(residual_ref, residual_out, sems.at[keep])
    extra.start()

    def put(side, low, values):
        for r in range(rows):
            for y in range(Y):
                for c in range(values.shape[1] // LANES):
                    start = ((side * Y + y) * Z * rows + r) * chunks + low // LANES + c
                    piece = values[(r * Y + y) * Z:(r * Y + y + 1) * Z, c * LANES:(c + 1) * LANES]
                    strips[pl.ds(start, Z, rows * chunks), :] = piece

    arrange(in_ref, wide, theirs_ref)
    put(0, 0, near_ref[...])
    for j, right_ref in enumerate(rights):
        put(1, j * block, dots(theirs_ref, right_ref))
    for copy in copies:
        copy.wait()
    for side, left_ref in enumerate((mine_ref, theirs_ref)):
        put(side, len(rights) * block, dots(left_ref, held))
        owner = lax.rem(core_ref[0] + side, CORE)
        size = Z * rows * chunks
        for y in range(Y):
            start = (side * Y + y) * size
            piece = strips[start:start + size, :].astype(out_ref.dtype)
            out_ref[y, :, owner] = piece.reshape(Z, rows * chunks, LANES)
    extra.wait()


def place_kernel(x_ref, residual_ref, ladder_ref, out_ref):
    groups, cores, _, columns = ladder_ref.shape
    block = columns // X
    for core in range(cores):
        for low, (step, side) in enumerate(HELD[core]):
            at = (lax.rem(x_ref[0] + step, X) * cores + side) * block
            for y in range(groups):
                place = pl.ds(pl.multiple_of(y * X * cores * block + at, block), block)
                ladder = ladder_ref[y, core, :, low * block:(low + 1) * block].astype(jnp.float32)
                total = residual_ref[:, place].astype(jnp.float32) + ladder
                out_ref[:, place] = total.astype(out_ref.dtype)


def shards(amplitudes, integrals, residual_in, kept_tiles):
    rows, tiles, width = amplitudes.shape
    keep = kept_tiles.shape[1]
    share = width // Z
    block = integrals.shape[1]
    x = lax.axis_index("x")
    core = lax.axis_index("c")

    first = lax.ppermute(integrals, ("x", "c"), SAME)
    second = lax.ppermute(integrals, ("x", "c"), CROSS)
    first, second = in_place(hold_kernel, (first, second), 2, [])
    third = lax.ppermute(first, ("x", "c"), SAME)

    outgoing = pick(kept_tiles, amplitudes)
    outgoing = outgoing.reshape(Y * Z, rows * keep, share // LANES, LANES)
    mine = lax.all_to_all(outgoing, GROUP, split_axis=0, concat_axis=0, tiled=True)
    left = jax.ShapeDtypeStruct((rows, keep, Y * Z, share), mine.dtype)
    theirs = lax.ppermute(mine, "c", SWAP)

    chunks = X * block // LANES
    all_shape = jax.ShapeDtypeStruct((Y, Z, CORE, rows * chunks, LANES), jnp.bfloat16)
    mine = mine.reshape(-1, LANES)
    wide = pltpu.VMEM((mine.shape[0] + SPARE, LANES), jnp.float32)
    near_shape = jax.ShapeDtypeStruct((rows * Y * Z, 3 * block), jnp.float32)
    near_blocks = (integrals, first, second)
    mine, near = call(near_kernel, (left, near_shape), (), (mine, *near_blocks), 1000, (), (wide,))
    where = x.astype(jnp.int32).reshape(1)
    which = core.astype(jnp.int32).reshape(1)
    out = jax.ShapeDtypeStruct(residual_in.shape, residual_in.dtype)
    room = (
        pltpu.VMEM(left.shape, left.dtype),
        pltpu.VMEM(third.shape, third.dtype),
        wide,
        pltpu.VMEM((CORE * Y * Z * rows * chunks + SPARE, LANES), jnp.float32),
        pltpu.SemaphoreType.DMA((keep + 1,)),
    )
    partial, residual = call(
        rest_kernel,
        (all_shape, out),
        (which, where),
        (mine, near, theirs.reshape(-1, LANES), *near_blocks),
        1000,
        (residual_in, third),
        room,
    )
    partial = partial.reshape(Y * CORE * Z, rows * chunks, LANES)
    returned = lax.all_to_all(partial, GROUP + ("c",), split_axis=0, concat_axis=0, tiled=True)
    returned = returned.reshape((2,) * 6 + (CORE, rows * chunks, LANES)).astype(jnp.float32)
    ladder = jnp.sum(returned, axis=(3, 4, 5)).astype(jnp.bfloat16)
    ladder = ladder.transpose(2, 1, 0, 3, 4, 5).reshape(Y, CORE, rows, X * block)
    return call(place_kernel, out, (where,), (residual, ladder), 1000)


def solution(mesh):
    fine = Mesh(mesh.devices.reshape(2, 2, 2, X, CORE, 2, 2, 2), AXES)
    in_specs = (
        P(AXES, None, None),
        P(None, AXES[:5], AXES[5:]),
        P(AXES, None),
        P(),
    )
    return jax.shard_map(
        shards, mesh=fine, in_specs=in_specs, out_specs=P(AXES, None), check_vma=False
    )
```

```python
import jax
import jax.numpy as jnp
from jax import lax
from jax.experimental import pallas as pl
from jax.experimental.pallas import tpu as pltpu
from jax.sharding import Mesh, PartitionSpec as P

Y, X, CORE, Z = 8, 4, 2, 8
LANES = 128
SWAP = ((0, 1), (1, 0))
SAME = tuple((2 * i + c, 2 * ((i + 1 - 2 * c) % X) + c) for i in range(X) for c in range(CORE))
CROSS = tuple((2 * i + 1 - c, 2 * ((i + 1 - 2 * c) % X) + c) for i in range(X) for c in range(CORE))
HELD = (((0, 0), (X - 1, 0), (X - 1, 1), (2, 0)), ((0, 1), (1, 1), (1, 0), (2, 1)))
AXES = ("y2", "y1", "y0", "x", "c", "z2", "z1", "z0")
GROUP = ("y0", "y1", "y2", "z0", "z1", "z2")
VMEM = pl.BlockSpec(memory_space=pltpu.VMEM)
SMEM = pl.BlockSpec(memory_space=pltpu.SMEM)
ANY = pl.BlockSpec(memory_space=pl.ANY)
GRANT = 32 * 1024 * 1024
SPARE = 64


def pick_kernel(kept_ref, amplitudes_ref, out_ref, held, sems):
    tiles, keep = kept_ref.shape
    rows = amplitudes_ref.shape[0]
    repeat = Y // tiles
    copies = []
    for a in range(tiles):
        for k in range(keep):
            tile = kept_ref[a, k]
            for r in range(rows):
                held[a, :, :, :, r * keep + k] = amplitudes_ref[r, tile]
        for i in range(repeat):
            y = a * repeat + i
            place = out_ref.at[y % 2, y // 2 % 2, y // 4]
            copies.append(pltpu.make_async_copy(held.at[a], place, sems.at[y]))
            copies[-1].start()
    for copy in copies:
        copy.wait()


def pick(kept_tiles, amplitudes):
    rows, tiles, width = amplitudes.shape
    keep = kept_tiles.shape[1]
    split = amplitudes.reshape(rows, tiles, 2, 2, 2, width // Z // LANES, LANES)
    split = split.transpose(0, 1, 4, 3, 2, 5, 6)
    shape = (Z, rows * keep, width // Z // LANES, LANES)
    return pl.pallas_call(
        pick_kernel,
        out_shape=jax.ShapeDtypeStruct((2,) * 6 + shape[1:], amplitudes.dtype),
        in_specs=[SMEM, VMEM],
        out_specs=ANY,
        scratch_shapes=[
            pltpu.VMEM((kept_tiles.shape[0], 2, 2, 2) + shape[1:], amplitudes.dtype),
            pltpu.SemaphoreType.DMA((Y,)),
        ],
        cost_estimate=pl.CostEstimate(flops=10**11, bytes_accessed=10**6, transcendentals=0),
        compiler_params=pltpu.CompilerParams(vmem_limit_bytes=GRANT),
    )(kept_tiles, split)


def call(kernel, out_shape, scalars, arrays, work, far=(), scratch=()):
    return pl.pallas_call(
        kernel,
        out_shape=out_shape,
        in_specs=[SMEM] * len(scalars) + [VMEM] * len(arrays) + [ANY] * len(far),
        out_specs=(VMEM,) * len(out_shape) if isinstance(out_shape, tuple) else VMEM,
        scratch_shapes=list(scratch),
        cost_estimate=pl.CostEstimate(flops=work, bytes_accessed=1000, transcendentals=0),
        compiler_params=pltpu.CompilerParams(vmem_limit_bytes=GRANT),
    )(*scalars, *arrays, *far)


def hold_kernel(a_ref, b_ref, a_out, b_out):
    pass


def in_place(kernel, arrays, kept, scratch):
    shapes = tuple(jax.ShapeDtypeStruct(a.shape, a.dtype) for a in arrays)
    return pl.pallas_call(
        kernel,
        out_shape=shapes,
        in_specs=[ANY] * len(arrays),
        out_specs=(ANY,) * len(arrays),
        scratch_shapes=scratch,
        input_output_aliases={i: i for i in range(kept)},
        cost_estimate=pl.CostEstimate(flops=10**11, bytes_accessed=10**6, transcendentals=0),
        compiler_params=pltpu.CompilerParams(vmem_limit_bytes=GRANT),
    )(*arrays)


def arrange(in_ref, wide, left_ref):
    rows, keep, peers, share = left_ref.shape
    chunks = share // LANES
    wide[:in_ref.shape[0], :] = in_ref[...].astype(jnp.float32)
    for r in range(rows):
        for k in range(keep):
            for c in range(chunks):
                at = pl.ds((r * keep + k) * chunks + c, peers, rows * keep * chunks)
                left_ref[r, k, :, c * LANES:(c + 1) * LANES] = wide[at, :].astype(left_ref.dtype)


def dots(left_ref, right_ref):
    rows, keep, peers, share = left_ref.shape
    total = None
    for k in range(keep):
        part = lax.dot_general(
            left_ref[:, k].reshape(rows * peers, share),
            right_ref[k],
            (((1,), (1,)), ((), ())),
            preferred_element_type=jnp.float32,
        )
        total = part if total is None else total + part
    return total


def near_kernel(in_ref, *refs):
    rights, (left_ref, out_ref, wide) = refs[:-3], refs[-3:]
    block = rights[0].shape[1]
    arrange(in_ref, wide, left_ref)
    for j, right_ref in enumerate(rights):
        out_ref[:, j * block:(j + 1) * block] = dots(left_ref, right_ref)


def rest_kernel(core_ref, _, mine_ref, near_ref, in_ref, *refs):
    rights = refs[:-9]
    residual_ref, third_ref, out_ref, residual_out, theirs_ref, held, wide, strips, sems = refs[-9:]
    rows, keep, _, _ = mine_ref.shape
    block = third_ref.shape[1]
    chunks = X * block // LANES
    copies = [pltpu.make_async_copy(third_ref.at[k], held.at[k], sems.at[k]) for k in range(keep)]
    for copy in copies:
        copy.start()
    extra = pltpu.make_async_copy(residual_ref, residual_out, sems.at[keep])
    extra.start()

    def put(side, low, values):
        for r in range(rows):
            for y in range(Y):
                for c in range(values.shape[1] // LANES):
                    start = ((side * Y + y) * Z * rows + r) * chunks + low // LANES + c
                    piece = values[(r * Y + y) * Z:(r * Y + y + 1) * Z, c * LANES:(c + 1) * LANES]
                    strips[pl.ds(start, Z, rows * chunks), :] = piece

    def finish(side):
        owner = lax.rem(core_ref[0] + side, CORE)
        size = Z * rows * chunks
        for y in range(Y):
            start = (side * Y + y) * size
            piece = strips[start:start + size, :].astype(out_ref.dtype)
            out_ref[y, :, owner] = piece.reshape(Z, rows * chunks, LANES)

    last = len(rights) - 1
    arrange(in_ref, wide, theirs_ref)
    put(0, 0, near_ref[...])
    for j in range(last):
        put(1, j * block, dots(theirs_ref, rights[j]))
    for copy in copies:
        copy.wait()
    put(0, len(rights) * block, dots(mine_ref, held))
    put(1, last * block, dots(theirs_ref, rights[last]))
    finish(0)
    put(1, len(rights) * block, dots(theirs_ref, held))
    finish(1)
    extra.wait()


def place_kernel(x_ref, residual_ref, ladder_ref, out_ref):
    groups, cores, _, columns = ladder_ref.shape
    block = columns // X
    for core in range(cores):
        for low, (step, side) in enumerate(HELD[core]):
            at = (lax.rem(x_ref[0] + step, X) * cores + side) * block
            for y in range(groups):
                place = pl.ds(pl.multiple_of(y * X * cores * block + at, block), block)
                ladder = ladder_ref[y, core, :, low * block:(low + 1) * block].astype(jnp.float32)
                total = residual_ref[:, place].astype(jnp.float32) + ladder
                out_ref[:, place] = total.astype(out_ref.dtype)


def shards(amplitudes, integrals, residual_in, kept_tiles):
    rows, tiles, width = amplitudes.shape
    keep = kept_tiles.shape[1]
    share = width // Z
    block = integrals.shape[1]
    x = lax.axis_index("x")
    core = lax.axis_index("c")

    first = lax.ppermute(integrals, ("x", "c"), SAME)
    second = lax.ppermute(integrals, ("x", "c"), CROSS)
    first, second = in_place(hold_kernel, (first, second), 2, [])
    third = lax.ppermute(first, ("x", "c"), SAME)

    outgoing = pick(kept_tiles, amplitudes)
    outgoing = outgoing.reshape(Y * Z, rows * keep, share // LANES, LANES)
    mine = lax.all_to_all(outgoing, GROUP, split_axis=0, concat_axis=0, tiled=True)
    left = jax.ShapeDtypeStruct((rows, keep, Y * Z, share), mine.dtype)
    theirs = lax.ppermute(mine, "c", SWAP)

    chunks = X * block // LANES
    all_shape = jax.ShapeDtypeStruct((Y, Z, CORE, rows * chunks, LANES), jnp.bfloat16)
    mine = mine.reshape(-1, LANES)
    wide = pltpu.VMEM((mine.shape[0] + SPARE, LANES), jnp.float32)
    near_shape = jax.ShapeDtypeStruct((rows * Y * Z, 3 * block), jnp.float32)
    near_blocks = (integrals, first, second)
    mine, near = call(near_kernel, (left, near_shape), (), (mine, *near_blocks), 1000, (), (wide,))
    where = x.astype(jnp.int32).reshape(1)
    which = core.astype(jnp.int32).reshape(1)
    out = jax.ShapeDtypeStruct(residual_in.shape, residual_in.dtype)
    room = (
        pltpu.VMEM(left.shape, left.dtype),
        pltpu.VMEM(third.shape, third.dtype),
        wide,
        pltpu.VMEM((CORE * Y * Z * rows * chunks + SPARE, LANES), jnp.float32),
        pltpu.SemaphoreType.DMA((keep + 1,)),
    )
    partial, residual = call(
        rest_kernel,
        (all_shape, out),
        (which, where),
        (mine, near, theirs.reshape(-1, LANES), *near_blocks),
        1000,
        (residual_in, third),
        room,
    )
    partial = partial.reshape(Y * CORE * Z, rows * chunks, LANES)
    returned = lax.all_to_all(partial, GROUP + ("c",), split_axis=0, concat_axis=0, tiled=True)
    returned = returned.reshape((2,) * 6 + (CORE, rows * chunks, LANES)).astype(jnp.float32)
    ladder = jnp.sum(returned, axis=(3, 4, 5)).astype(jnp.bfloat16)
    ladder = ladder.transpose(2, 1, 0, 3, 4, 5).reshape(Y, CORE, rows, X * block)
    return call(place_kernel, out, (where,), (residual, ladder), 1000)


def solution(mesh):
    fine = Mesh(mesh.devices.reshape(2, 2, 2, X, CORE, 2, 2, 2), AXES)
    in_specs = (
        P(AXES, None, None),
        P(None, AXES[:5], AXES[5:]),
        P(AXES, None),
        P(),
    )
    return jax.shard_map(
        shards, mesh=fine, in_specs=in_specs, out_specs=P(AXES, None), check_vma=False
    )
```

```python
import jax
import jax.numpy as jnp
from jax import lax
from jax.experimental import pallas as pl
from jax.experimental.pallas import tpu as pltpu
from jax.sharding import Mesh, PartitionSpec as P

Y, X, CORE, Z = 8, 4, 2, 8
LANES = 128
SWAP = ((0, 1), (1, 0))
SAME = tuple((2 * i + c, 2 * ((i + 1 - 2 * c) % X) + c) for i in range(X) for c in range(CORE))
CROSS = tuple((2 * i + 1 - c, 2 * ((i + 1 - 2 * c) % X) + c) for i in range(X) for c in range(CORE))
HELD = (((0, 0), (X - 1, 0), (X - 1, 1), (2, 0)), ((0, 1), (1, 1), (1, 0), (2, 1)))
AXES = ("y2", "y1", "y0", "x", "c", "z2", "z1", "z0")
GROUP = ("y0", "y1", "y2", "z1", "z0", "z2")
VMEM = pl.BlockSpec(memory_space=pltpu.VMEM)
SMEM = pl.BlockSpec(memory_space=pltpu.SMEM)
ANY = pl.BlockSpec(memory_space=pl.ANY)
GRANT = 32 * 1024 * 1024
SPARE = 64


def pick_kernel(kept_ref, amplitudes_ref, out_ref, held, sems):
    tiles, keep = kept_ref.shape
    rows = amplitudes_ref.shape[0]
    repeat = Y // tiles
    copies = []
    for a in range(tiles):
        for k in range(keep):
            tile = kept_ref[a, k]
            for r in range(rows):
                held[a, :, :, :, r * keep + k] = amplitudes_ref[r, tile]
        for i in range(repeat):
            y = a * repeat + i
            place = out_ref.at[y % 2, y // 2 % 2, y // 4]
            copies.append(pltpu.make_async_copy(held.at[a], place, sems.at[y]))
            copies[-1].start()
    for copy in copies:
        copy.wait()


def pick(kept_tiles, amplitudes):
    rows, tiles, width = amplitudes.shape
    keep = kept_tiles.shape[1]
    split = amplitudes.reshape(rows, tiles, 2, 2, 2, width // Z // LANES, LANES)
    split = split.transpose(0, 1, 3, 4, 2, 5, 6)
    shape = (Z, rows * keep, width // Z // LANES, LANES)
    return pl.pallas_call(
        pick_kernel,
        out_shape=jax.ShapeDtypeStruct((2,) * 6 + shape[1:], amplitudes.dtype),
        in_specs=[SMEM, VMEM],
        out_specs=ANY,
        scratch_shapes=[
            pltpu.VMEM((kept_tiles.shape[0], 2, 2, 2) + shape[1:], amplitudes.dtype),
            pltpu.SemaphoreType.DMA((Y,)),
        ],
        cost_estimate=pl.CostEstimate(flops=10**11, bytes_accessed=10**6, transcendentals=0),
        compiler_params=pltpu.CompilerParams(vmem_limit_bytes=GRANT),
    )(kept_tiles, split)


def call(kernel, out_shape, scalars, arrays, work, far=(), scratch=()):
    return pl.pallas_call(
        kernel,
        out_shape=out_shape,
        in_specs=[SMEM] * len(scalars) + [VMEM] * len(arrays) + [ANY] * len(far),
        out_specs=(VMEM,) * len(out_shape) if isinstance(out_shape, tuple) else VMEM,
        scratch_shapes=list(scratch),
        cost_estimate=pl.CostEstimate(flops=work, bytes_accessed=1000, transcendentals=0),
        compiler_params=pltpu.CompilerParams(vmem_limit_bytes=GRANT),
    )(*scalars, *arrays, *far)


def hold_kernel(a_ref, b_ref, a_out, b_out):
    pass


def in_place(kernel, arrays, kept, scratch):
    shapes = tuple(jax.ShapeDtypeStruct(a.shape, a.dtype) for a in arrays)
    return pl.pallas_call(
        kernel,
        out_shape=shapes,
        in_specs=[ANY] * len(arrays),
        out_specs=(ANY,) * len(arrays),
        scratch_shapes=scratch,
        input_output_aliases={i: i for i in range(kept)},
        cost_estimate=pl.CostEstimate(flops=10**11, bytes_accessed=10**6, transcendentals=0),
        compiler_params=pltpu.CompilerParams(vmem_limit_bytes=GRANT),
    )(*arrays)


def arrange(in_ref, wide, left_ref):
    rows, keep, peers, share = left_ref.shape
    chunks = share // LANES
    wide[:in_ref.shape[0], :] = in_ref[...].astype(jnp.float32)
    for r in range(rows):
        for k in range(keep):
            for c in range(chunks):
                at = pl.ds((r * keep + k) * chunks + c, peers, rows * keep * chunks)
                left_ref[r, k, :, c * LANES:(c + 1) * LANES] = wide[at, :].astype(left_ref.dtype)


def dots(left_ref, right_ref):
    rows, keep, peers, share = left_ref.shape
    total = None
    for k in range(keep):
        part = lax.dot_general(
            left_ref[:, k].reshape(rows * peers, share),
            right_ref[k],
            (((1,), (1,)), ((), ())),
            preferred_element_type=jnp.float32,
        )
        total = part if total is None else total + part
    return total


def near_kernel(in_ref, *refs):
    rights, (left_ref, out_ref, wide) = refs[:-3], refs[-3:]
    block = rights[0].shape[1]
    arrange(in_ref, wide, left_ref)
    for j, right_ref in enumerate(rights):
        out_ref[:, j * block:(j + 1) * block] = dots(left_ref, right_ref)


def rest_kernel(core_ref, _, mine_ref, near_ref, in_ref, *refs):
    rights = refs[:-9]
    residual_ref, third_ref, out_ref, residual_out, theirs_ref, held, wide, strips, sems = refs[-9:]
    rows, keep, _, _ = mine_ref.shape
    block = third_ref.shape[1]
    chunks = X * block // LANES
    copies = [pltpu.make_async_copy(third_ref.at[k], held.at[k], sems.at[k]) for k in range(keep)]
    for copy in copies:
        copy.start()
    extra = pltpu.make_async_copy(residual_ref, residual_out, sems.at[keep])
    extra.start()

    def put(side, low, values):
        for r in range(rows):
            for y in range(Y):
                for c in range(values.shape[1] // LANES):
                    start = ((side * Y + y) * Z * rows + r) * chunks + low // LANES + c
                    piece = values[(r * Y + y) * Z:(r * Y + y + 1) * Z, c * LANES:(c + 1) * LANES]
                    strips[pl.ds(start, Z, rows * chunks), :] = piece

    arrange(in_ref, wide, theirs_ref)
    put(0, 0, near_ref[...])
    for j, right_ref in enumerate(rights):
        put(1, j * block, dots(theirs_ref, right_ref))
    for copy in copies:
        copy.wait()
    for side, left_ref in enumerate((mine_ref, theirs_ref)):
        put(side, len(rights) * block, dots(left_ref, held))
        owner = lax.rem(core_ref[0] + side, CORE)
        size = Z * rows * chunks
        for y in range(Y):
            start = (side * Y + y) * size
            piece = strips[start:start + size, :].astype(out_ref.dtype)
            out_ref[y, :, owner] = piece.reshape(Z, rows * chunks, LANES)
    extra.wait()


def place_kernel(x_ref, residual_ref, ladder_ref, out_ref):
    groups, cores, _, columns = ladder_ref.shape
    block = columns // X
    for core in range(cores):
        for low, (step, side) in enumerate(HELD[core]):
            at = (lax.rem(x_ref[0] + step, X) * cores + side) * block
            for y in range(groups):
                place = pl.ds(pl.multiple_of(y * X * cores * block + at, block), block)
                ladder = ladder_ref[y, core, :, low * block:(low + 1) * block].astype(jnp.float32)
                total = residual_ref[:, place].astype(jnp.float32) + ladder
                out_ref[:, place] = total.astype(out_ref.dtype)


def shards(amplitudes, integrals, residual_in, kept_tiles):
    rows, tiles, width = amplitudes.shape
    keep = kept_tiles.shape[1]
    share = width // Z
    block = integrals.shape[1]
    x = lax.axis_index("x")
    core = lax.axis_index("c")

    first = lax.ppermute(integrals, ("x", "c"), SAME)
    second = lax.ppermute(integrals, ("x", "c"), CROSS)
    first, second = in_place(hold_kernel, (first, second), 2, [])
    third = lax.ppermute(first, ("x", "c"), SAME)

    outgoing = pick(kept_tiles, amplitudes)
    outgoing = outgoing.reshape(Y * Z, rows * keep, share // LANES, LANES)
    mine = lax.all_to_all(outgoing, GROUP, split_axis=0, concat_axis=0, tiled=True)
    left = jax.ShapeDtypeStruct((rows, keep, Y * Z, share), mine.dtype)
    theirs = lax.ppermute(mine, "c", SWAP)

    chunks = X * block // LANES
    all_shape = jax.ShapeDtypeStruct((Y, Z, CORE, rows * chunks, LANES), jnp.bfloat16)
    mine = mine.reshape(-1, LANES)
    wide = pltpu.VMEM((mine.shape[0] + SPARE, LANES), jnp.float32)
    near_shape = jax.ShapeDtypeStruct((rows * Y * Z, 3 * block), jnp.float32)
    near_blocks = (integrals, first, second)
    mine, near = call(near_kernel, (left, near_shape), (), (mine, *near_blocks), 1000, (), (wide,))
    where = x.astype(jnp.int32).reshape(1)
    which = core.astype(jnp.int32).reshape(1)
    out = jax.ShapeDtypeStruct(residual_in.shape, residual_in.dtype)
    room = (
        pltpu.VMEM(left.shape, left.dtype),
        pltpu.VMEM(third.shape, third.dtype),
        wide,
        pltpu.VMEM((CORE * Y * Z * rows * chunks + SPARE, LANES), jnp.float32),
        pltpu.SemaphoreType.DMA((keep + 1,)),
    )
    partial, residual = call(
        rest_kernel,
        (all_shape, out),
        (which, where),
        (mine, near, theirs.reshape(-1, LANES), *near_blocks),
        1000,
        (residual_in, third),
        room,
    )
    partial = partial.reshape(Y * CORE * Z, rows * chunks, LANES)
    returned = lax.all_to_all(partial, GROUP + ("c",), split_axis=0, concat_axis=0, tiled=True)
    returned = returned.reshape((2,) * 6 + (CORE, rows * chunks, LANES)).astype(jnp.float32)
    ladder = jnp.sum(returned, axis=(3, 4, 5)).astype(jnp.bfloat16)
    ladder = ladder.transpose(2, 1, 0, 3, 4, 5).reshape(Y, CORE, rows, X * block)
    return call(place_kernel, out, (where,), (residual, ladder), 1000)


def solution(mesh):
    fine = Mesh(mesh.devices.reshape(2, 2, 2, X, CORE, 2, 2, 2), AXES)
    in_specs = (
        P(AXES, None, None),
        P(None, AXES[:5], AXES[5:]),
        P(AXES, None),
        P(),
    )
    return jax.shard_map(
        shards, mesh=fine, in_specs=in_specs, out_specs=P(AXES, None), check_vma=False
    )
```
